32 devices in a mesh: graph: 8 (over z, y), feat: 4 (over x, core).
Axes of the slice: x: 2, y: 2, z: 4, core: 2. Of those that a mesh axis runs over, the one named last changes fastest.
Arguments:
- features: bfloat16 [16384, 1024], P('graph', 'feat'), may hold values from -6 to 6
- w_self: bfloat16 [1024, 1024], replicated, may hold values from -0.1875 to 0.1875
- w_neigh: bfloat16 [1024, 1024], replicated, may hold values from -0.1875 to 0.1875
- adjacency: bfloat16 [256, 128, 128], P('graph'), may hold values from 0 to 1.5, as said below
- block_source: int32 [256], P('graph'), may hold values from 0 to 15
- block_to_slot: int32 [256], P('graph'), may hold values from 0 to 15
- send_rows: int32 [8, 8, 256], P('graph'), may hold values from 0 to 2047
- send_counts: int32 [8, 8], P('graph'), may hold values from 64 to 256, as said below
- degree: int32 [16384], P('graph'), may hold values from 8 to 32
- cotangent: bfloat16 [16384, 1024], P('graph', 'feat'), may hold values from -6 to 6
Outputs:
- hidden_out: bfloat16 [16384, 1024], P('graph', 'feat')
- grad_features: bfloat16 [16384, 1024], P('graph', 'feat')
- grad_self: float32 [1024, 1024], P('feat')
- grad_neigh: float32 [1024, 1024], P('feat')
The draws below stay inside these ranges and needn't reach their ends.
Inputs may be any that keep to these rules, and one draw needn't show every extreme that they name: Slots 0 to send_counts[p, q] - 1 from p to q are live; in every draw some partition receives 256 live slots from every partition. `adjacency`: edge weights; a block is mostly zeros.
All inputs are finite; a program needn't handle non-finite values.
Results may differ from the reference program's by a relative error of at most 0.0066.
Values may be sent and summed in bfloat16 or wider, within the bound.
A program may use at most 128 MiB of HBM per device.

```python
import jax
import jax.numpy as jnp
from jax import lax

D = 1024
NODE_DEV = 2048
BLK = 128
PARTITIONS = 8
NODES = 16384
CAP = 256
SLOT_BLOCK_COUNT = 16
NBLK = 32
ADJACENCY_BLOCKS = 256


def draw_adjacency(key, part):
    key_mask = jax.random.fold_in(key, 11)
    key_value = jax.random.fold_in(key, 12)
    shape = (ADJACENCY_BLOCKS, BLK, BLK)
    present = jax.random.bernoulli(key_mask, 0.3, shape)
    values = jax.random.uniform(key_value, shape, jnp.float32, 0.5, 1.5)
    return jnp.where(present, values, jnp.float32(0.0)).astype(jnp.bfloat16)


def draw_send_counts(key, part):
    part_count = NODES // NODE_DEV
    key_counts = jax.random.fold_in(key, 21)
    key_full = jax.random.fold_in(key, 22)
    counts = jax.random.randint(key_counts, (part_count, part_count), CAP // 4, CAP + 1, dtype=jnp.int32)
    full_owner = jax.random.randint(key_full, (), 0, part_count, dtype=jnp.int32)
    column = jnp.arange(part_count, dtype=jnp.int32)[None, :] == full_owner
    return jnp.where(column, jnp.int32(CAP), counts).astype(jnp.int32)


def with_ends(drawn, stream_key, low, high):
    spot = [jax.random.randint(jax.random.fold_in(stream_key, axis), (), 0, length) for axis, length in enumerate(drawn.shape)]
    longest = drawn.shape.index(max(drawn.shape))
    neighbour = spot[:longest] + [(spot[longest] + 1) % drawn.shape[longest]] + spot[longest + 1:]
    return drawn.at[tuple(spot)].set(low).at[tuple(neighbour)].set(high)


def level_of(rng, dims, cuts, low, top_value):
    loudness, own = 1.0, jax.random.fold_in(rng, 6)
    for axis_at, shards_of in cuts:
        heights = jnp.exp(jax.random.uniform(jax.random.fold_in(own, axis_at), (shards_of,), jnp.float32, low / len(cuts), top_value / len(cuts)))
        loudness = loudness * jnp.repeat(heights, dims[axis_at] // shards_of).reshape([-1 if axis == axis_at else 1 for axis in range(len(dims))])
    return loudness


def noise(rng, shape, deviation, bound, pieces=(), kind=jnp.bfloat16):
    result = jax.random.normal(rng, shape, jnp.float32) * deviation
    if len(pieces) > 0:
        result = level_of(rng, shape, pieces, -0.22, 0.18) * result
    return jnp.clip(result, min=-bound, max=bound).astype(kind)


def setup_inputs(seed: int = 0) -> dict:
    arg_keys = jax.random.split(jax.random.key(seed), 11)
    return {
        "features": noise(arg_keys[0], (NODES, D), 1.0, 6.0, ((0, 8), (1, 4))),
        "w_self": noise(arg_keys[1], (D, D), D ** -0.5, 0.1875),
        "w_neigh": noise(arg_keys[2], (D, D), D ** -0.5, 0.1875),
        "adjacency": draw_adjacency(jax.random.fold_in(arg_keys[10], 71), 0),
        "block_source": with_ends(jax.random.randint(arg_keys[4], (ADJACENCY_BLOCKS,), 0, NODE_DEV // BLK), jax.random.fold_in(arg_keys[4], 1), 0, (NODE_DEV // BLK) - 1).astype(jnp.int32),
        "block_to_slot": with_ends(jax.random.randint(arg_keys[5], (ADJACENCY_BLOCKS,), 0, SLOT_BLOCK_COUNT), jax.random.fold_in(arg_keys[5], 1), 0, SLOT_BLOCK_COUNT - 1).astype(jnp.int32),
        "send_rows": with_ends(jax.random.randint(arg_keys[6], (PARTITIONS, PARTITIONS, CAP), 0, NODE_DEV), jax.random.fold_in(arg_keys[6], 1), 0, NODE_DEV - 1).astype(jnp.int32),
        "send_counts": draw_send_counts(jax.random.fold_in(arg_keys[10], 71), 0),
        "degree": with_ends(jax.random.randint(arg_keys[8], (NODES,), 8, 33), jax.random.fold_in(arg_keys[8], 1), 8, 32).astype(jnp.int32),
        "cotangent": noise(arg_keys[9], (NODES, D), 1.0, 6.0, ((0, 8), (1, 4))),
    }


def silu_slope(values):
    sig = jax.nn.sigmoid(values)
    return sig * (1.0 + values * (1.0 - sig))


def reference(features, w_self, w_neigh, adjacency, block_source, block_to_slot, send_rows, send_counts, degree, cotangent):
    part_count = PARTITIONS
    source_count = NODE_DEV // BLK
    slot_total = SLOT_BLOCK_COUNT
    feat_blocks = features.reshape(part_count, source_count, BLK, D)
    adj_parts = adjacency.reshape(part_count, NBLK, BLK, BLK)
    source_parts = block_source.reshape(part_count, NBLK).astype(jnp.int32)
    slot_parts = block_to_slot.reshape(part_count, NBLK).astype(jnp.int32)
    slot_position = jnp.arange(CAP, dtype=jnp.int32)
    is_live = slot_position[None, None, :] < send_counts[:, :, None]
    owner_base = (jnp.arange(part_count, dtype=jnp.int32) * NODE_DEV)[None, :, None]
    targets = jnp.where(is_live, owner_base + send_rows.astype(jnp.int32), NODES).astype(jnp.int32)

    def forward_step(running, inputs):
        own_blocks, adj_here, source_local, slot_here, target_local, live_here = inputs
        picked = own_blocks[source_local]
        prods = jnp.einsum("kij,kjd->kid", adj_here.astype(jnp.float32), picked.astype(jnp.float32))
        slot_sums = jax.ops.segment_sum(prods, slot_here, num_segments=slot_total)
        slot_sums = slot_sums.reshape(part_count, CAP, D)
        partial_rows = jnp.where(live_here[:, :, None], slot_sums, 0.0).astype(jnp.bfloat16)
        running = running.at[target_local.reshape(-1)].add(partial_rows.reshape(-1, D).astype(jnp.float32), mode="drop")
        return running, None

    neighbor_sum, unused = lax.scan(forward_step, jnp.zeros((NODES, D), jnp.float32),
                                    (feat_blocks, adj_parts, source_parts, slot_parts, targets, is_live))
    degrees = degree.astype(jnp.float32)[:, None]
    neighbor_mean = (neighbor_sum / degrees).astype(jnp.bfloat16)
    pre_act = jnp.dot(features, w_self, preferred_element_type=jnp.float32) + jnp.dot(neighbor_mean, w_neigh, preferred_element_type=jnp.float32)
    hidden_out = jax.nn.silu(pre_act).astype(jnp.bfloat16)
    grad_pre = (cotangent.astype(jnp.float32) * silu_slope(pre_act)).astype(jnp.bfloat16)
    grad_self = jnp.dot(features.T, grad_pre, preferred_element_type=jnp.float32)
    grad_neigh = jnp.dot(neighbor_mean.T, grad_pre, preferred_element_type=jnp.float32)
    self_part = jnp.dot(grad_pre, w_self.T, preferred_element_type=jnp.float32)
    back_rows = (jnp.dot(grad_pre, w_neigh.T, preferred_element_type=jnp.float32) / degrees).astype(jnp.bfloat16)
    back_padded = jnp.concatenate([back_rows, jnp.zeros((1, D), jnp.bfloat16)], axis=0)

    def backward_step(inputs):
        adj_here, source_local, slot_here, target_local = inputs
        returned = back_padded[target_local].reshape(slot_total, BLK, D)
        chosen = returned[slot_here]
        contrib = jnp.einsum("kij,kid->kjd", adj_here.astype(jnp.float32), chosen.astype(jnp.float32))
        summed = jax.ops.segment_sum(contrib, source_local, num_segments=source_count)
        return summed.reshape(NODE_DEV, D)

    neigh_part = lax.map(backward_step, (adj_parts, source_parts, slot_parts, targets))
    grad_features = (self_part + neigh_part.reshape(NODES, D)).astype(jnp.bfloat16)
    return (hidden_out, grad_features, grad_self, grad_neigh)
```

```python
import functools

import jax
import jax.numpy as jnp
from jax import lax
from jax.experimental import pallas as pl
from jax.experimental.pallas import tpu as pltpu
from jax.sharding import PartitionSpec as P

SMEM = pltpu.SMEM
VMEM = pltpu.VMEM
GROUP = 4


def silu_slope(values):
    sig = jax.nn.sigmoid(values)
    return sig * (1.0 + values * (1.0 - sig))


def collect_kernel(source_ref, slot_ref, count_ref, adj_ref, feat_ref, out_ref, acc):
    blocks, block, _ = adj_ref.shape
    slot_total = out_ref.shape[0]
    halves = slot_total // count_ref.shape[1]
    acc[...] = jnp.zeros_like(acc)

    def add(step, carry):
        prods = []
        for j in range(GROUP):
            k = step * GROUP + j
            rows = pl.ds(pl.multiple_of(source_ref[k] * block, block), block)
            prods.append(jnp.dot(adj_ref[k], feat_ref[rows, :], preferred_element_type=jnp.float32))
        for j in range(GROUP):
            acc[slot_ref[step * GROUP + j]] += prods[j]
        return carry

    lax.fori_loop(0, blocks // GROUP, add, 0)

    def finish(s, carry):
        limit = count_ref[0, s // halves] - (s % halves) * block
        rows = lax.broadcasted_iota(jnp.int32, out_ref.shape[1:], 0)
        out_ref[s] = jnp.where(rows < limit, acc[s], 0.0).astype(jnp.bfloat16)
        return carry

    lax.fori_loop(0, slot_total, finish, 0)


def collect(block_source, block_to_slot, send_counts, adjacency, features, slot_total):
    blocks, block, _ = adjacency.shape
    shape = (slot_total, block, features.shape[1])
    return pl.pallas_call(
        collect_kernel,
        out_shape=jax.ShapeDtypeStruct(shape, jnp.bfloat16),
        in_specs=[pl.BlockSpec(memory_space=SMEM)] * 3 + [pl.BlockSpec(memory_space=VMEM)] * 2,
        out_specs=pl.BlockSpec(memory_space=VMEM),
        scratch_shapes=[pltpu.VMEM(shape, jnp.float32)],
        compiler_params=pltpu.CompilerParams(vmem_limit_bytes=32 * 2**20),
        name="collect",
    )(block_source, block_to_slot, send_counts, adjacency, features)


def spread_kernel(source_ref, slot_ref, adj_ref, ret_ref, grad_ref, w_ref, out_ref, acc):
    blocks, block, _ = adj_ref.shape
    sources = out_ref.shape[0] // block

    def start(b, carry):
        rows = pl.ds(pl.multiple_of(b * block, block), block)
        acc[b] = lax.dot_general(
            grad_ref[rows, :], w_ref[...], (((1,), (1,)), ((), ())),
            preferred_element_type=jnp.float32,
        )
        return carry

    lax.fori_loop(0, sources, start, 0)

    def add(step, carry):
        prods = []
        for j in range(GROUP):
            k = step * GROUP + j
            prods.append(lax.dot_general(
                adj_ref[k], ret_ref[slot_ref[k]], (((0,), (0,)), ((), ())),
                preferred_element_type=jnp.float32,
            ))
        for j in range(GROUP):
            acc[source_ref[step * GROUP + j]] += prods[j]
        return carry

    lax.fori_loop(0, blocks // GROUP, add, 0)

    def finish(b, carry):
        rows = pl.ds(pl.multiple_of(b * block, block), block)
        out_ref[rows, :] = acc[b].astype(jnp.bfloat16)
        return carry

    lax.fori_loop(0, sources, finish, 0)


def spread(block_source, block_to_slot, adjacency, returned, grad_full, self_rows):
    blocks, block, _ = adjacency.shape
    nodes = grad_full.shape[0]
    cols = returned.shape[2]
    return pl.pallas_call(
        spread_kernel,
        out_shape=jax.ShapeDtypeStruct((nodes, cols), jnp.bfloat16),
        in_specs=[pl.BlockSpec(memory_space=SMEM)] * 2 + [pl.BlockSpec(memory_space=VMEM)] * 4,
        out_specs=pl.BlockSpec(memory_space=VMEM),
        scratch_shapes=[pltpu.VMEM((nodes // block, block, cols), jnp.float32)],
        compiler_params=pltpu.CompilerParams(vmem_limit_bytes=40 * 2**20),
        name="spread",
    )(block_source, block_to_slot, adjacency, returned, grad_full, self_rows)


def on_device(
    features,
    w_self,
    w_neigh,
    adjacency,
    block_source,
    block_to_slot,
    send_rows,
    send_counts,
    degree,
    cotangent,
):
    node_rows, feat_cols = features.shape
    part_count = lax.axis_size("graph")
    block_size = adjacency.shape[1]
    slot_cap = send_rows.shape[2]
    slot_total = part_count * slot_cap // block_size
    column_start = lax.axis_index("feat") * feat_cols
    feat_full = lax.all_gather(features, "feat", axis=1, tiled=True)
    outgoing = collect(block_source, block_to_slot, send_counts, adjacency, features, slot_total)
    is_live = jnp.arange(slot_cap, dtype=jnp.int32)[None, :] < send_counts[0][:, None]
    row_ids = jnp.where(is_live, send_rows[0], -1)
    incoming_ids = lax.all_to_all(row_ids, "graph", split_axis=0, concat_axis=0, tiled=True)
    incoming = lax.all_to_all(
        outgoing.reshape(part_count, slot_cap, feat_cols), "graph", split_axis=0, concat_axis=0, tiled=True
    )
    targets = incoming_ids.reshape(-1)
    match = (jnp.arange(node_rows, dtype=jnp.int32)[:, None] == targets[None, :]).astype(jnp.bfloat16)
    neighbor_sum = jnp.dot(match, incoming.reshape(-1, feat_cols), preferred_element_type=jnp.float32)
    degrees = degree.astype(jnp.float32)[:, None]
    neighbor_mean = (neighbor_sum / degrees).astype(jnp.bfloat16)
    agg_full = lax.all_gather(neighbor_mean, "feat", axis=1, tiled=True)
    self_rows = lax.dynamic_slice_in_dim(w_self, column_start, feat_cols, 0)
    neigh_rows = lax.dynamic_slice_in_dim(w_neigh, column_start, feat_cols, 0)
    self_cols = lax.dynamic_slice_in_dim(w_self, column_start, feat_cols, 1)
    neigh_cols = lax.dynamic_slice_in_dim(w_neigh, column_start, feat_cols, 1)
    pre_act = jnp.dot(feat_full, self_cols, preferred_element_type=jnp.float32) + jnp.dot(
        agg_full, neigh_cols, preferred_element_type=jnp.float32
    )
    hidden_out = jax.nn.silu(pre_act).astype(jnp.bfloat16)
    grad_pre = (cotangent.astype(jnp.float32) * silu_slope(pre_act)).astype(jnp.bfloat16)
    grad_full = lax.all_gather(grad_pre, "feat", axis=1, tiled=True)
    local_self = lax.dot_general(
        features, grad_full, (((0,), (0,)), ((), ())), preferred_element_type=jnp.float32
    )
    local_neigh = lax.dot_general(
        neighbor_mean, grad_full, (((0,), (0,)), ((), ())), preferred_element_type=jnp.float32
    )
    grad_self, grad_neigh = lax.psum((local_self, local_neigh), "graph")
    back_rows = (
        lax.dot_general(
            grad_full, neigh_rows, (((1,), (1,)), ((), ())), preferred_element_type=jnp.float32
        )
        / degrees
    ).astype(jnp.bfloat16)
    sending_back = lax.dot_general(
        match, back_rows, (((0,), (0,)), ((), ())), preferred_element_type=jnp.float32
    ).astype(jnp.bfloat16)
    returned = lax.all_to_all(
        sending_back.reshape(part_count, slot_cap, feat_cols), "graph", split_axis=0, concat_axis=0, tiled=True
    )
    grad_features = spread(
        block_source, block_to_slot, adjacency,
        returned.reshape(slot_total, block_size, feat_cols), grad_full, self_rows,
    )
    return (hidden_out, grad_features, grad_self, grad_neigh)


def solution(mesh):
    placed = (
        P("graph", "feat"),
        P(),
        P(),
        P("graph", None, None),
        P("graph"),
        P("graph"),
        P("graph", None, None),
        P("graph", None),
        P("graph"),
        P("graph", "feat"),
    )
    return jax.shard_map(
        on_device,
        mesh=mesh,
        in_specs=placed,
        out_specs=(P("graph", "feat"), P("graph", "feat"), P("feat", None), P("feat", None)),
        check_vma=False,
    )
```

```python
import functools

import jax
import jax.numpy as jnp
from jax import lax
from jax.experimental import pallas as pl
from jax.experimental.pallas import tpu as pltpu
from jax.sharding import PartitionSpec as P

SMEM = pltpu.SMEM
VMEM = pltpu.VMEM
MESH = pl.DeviceIdType.MESH
GROUP = 4
CHUNKS = 4


def collect_kernel(source_ref, slot_ref, count_ref, adj_ref, feat_ref, out_ref, acc):
    blocks, block, _ = adj_ref.shape
    slot_total = out_ref.shape[0]
    halves = slot_total // count_ref.shape[1]
    acc[...] = jnp.zeros_like(acc)

    def add(step, carry):
        prods = []
        for j in range(GROUP):
            k = step * GROUP + j
            rows = pl.ds(pl.multiple_of(source_ref[k] * block, block), block)
            prods.append(jnp.dot(adj_ref[k], feat_ref[rows, :], preferred_element_type=jnp.float32))
        for j in range(GROUP):
            acc[slot_ref[step * GROUP + j]] += prods[j]
        return carry

    lax.fori_loop(0, blocks // GROUP, add, 0)

    def finish(s, carry):
        limit = count_ref[0, s // halves] - (s % halves) * block
        rows = lax.broadcasted_iota(jnp.int32, out_ref.shape[1:], 0)
        out_ref[s] = jnp.where(rows < limit, acc[s], 0.0).astype(jnp.bfloat16)
        return carry

    lax.fori_loop(0, slot_total, finish, 0)


def collect(block_source, block_to_slot, send_counts, adjacency, features, slot_total):
    blocks, block, _ = adjacency.shape
    shape = (slot_total, block, features.shape[1])
    return pl.pallas_call(
        collect_kernel,
        out_shape=jax.ShapeDtypeStruct(shape, jnp.bfloat16),
        in_specs=[pl.BlockSpec(memory_space=SMEM)] * 3 + [pl.BlockSpec(memory_space=VMEM)] * 2,
        out_specs=pl.BlockSpec(memory_space=VMEM),
        scratch_shapes=[pltpu.VMEM(shape, jnp.float32)],
        compiler_params=pltpu.CompilerParams(vmem_limit_bytes=32 * 2**20),
        name="collect",
    )(block_source, block_to_slot, send_counts, adjacency, features)


def spread_kernel(source_ref, slot_ref, adj_ref, ret_ref, start_ref, out_ref, acc):
    blocks, block, _ = adj_ref.shape
    sources = out_ref.shape[0] // block
    acc[...] = start_ref[...]

    def add(step, carry):
        prods = []
        for j in range(GROUP):
            k = step * GROUP + j
            prods.append(lax.dot_general(
                adj_ref[k], ret_ref[slot_ref[k]], (((0,), (0,)), ((), ())),
                preferred_element_type=jnp.float32,
            ))
        for j in range(GROUP):
            acc[source_ref[step * GROUP + j]] += prods[j]
        return carry

    lax.fori_loop(0, blocks // GROUP, add, 0)

    def finish(b, carry):
        rows = pl.ds(pl.multiple_of(b * block, block), block)
        out_ref[rows, :] = acc[b].astype(jnp.bfloat16)
        return carry

    lax.fori_loop(0, sources, finish, 0)


def spread(block_source, block_to_slot, adjacency, returned, self_grad):
    blocks, block, _ = adjacency.shape
    nodes, cols = self_grad.shape
    shape = (nodes // block, block, cols)
    return pl.pallas_call(
        spread_kernel,
        out_shape=jax.ShapeDtypeStruct((nodes, cols), jnp.bfloat16),
        in_specs=[pl.BlockSpec(memory_space=SMEM)] * 2 + [pl.BlockSpec(memory_space=VMEM)] * 3,
        out_specs=pl.BlockSpec(memory_space=VMEM),
        scratch_shapes=[pltpu.VMEM(shape, jnp.float32)],
        compiler_params=pltpu.CompilerParams(vmem_limit_bytes=32 * 2**20),
        name="spread",
    )(block_source, block_to_slot, adjacency, returned, self_grad.reshape(shape))


def layer_kernel(
    parts, feats,
    out_blocks, out_ids, feat_ref, deg_ref, cot_ref, w_self, w_neigh,
    hidden_ref, returned_ref, self_grad_ref, grad_self_ref, grad_neigh_ref,
    in_blocks, in_ids, sum_ref, pre_ref, feat_full, agg_full, grad_full, back_ref, back_out, back_in,
    self_cols, neigh_cols, self_rows, neigh_rows, weight_acc,
    y_out, y_in, z_out, z_in, z_all, y_all,
    a_send, a_recv, i_send, i_recv, r_send, r_recv, w_sem,
    gx_send, gs_send, gr_send, g_recv,
    ys_send, ys_recv, zs_send, zs_recv, za_send, za_recv, ya_send, ya_recv,
):
    g, f = lax.axis_index("graph"), lax.axis_index("feat")
    chips = feats // 2
    ys = chips
    zs = parts // ys
    x, core = f // 2, f % 2
    sibling = x * 2 + 1 - core
    z, y = g // ys, g % ys
    nodes, cols = feat_ref.shape
    width = feats * cols
    chunk = nodes // CHUNKS

    def remote(src, dst, send, recv, graph_to, feat_to):
        return pltpu.make_async_remote_copy(
            src_ref=src, dst_ref=dst, send_sem=send, recv_sem=recv,
            device_id=(graph_to, feat_to), device_id_type=MESH,
        )

    def span(c):
        return pl.ds(pl.multiple_of(c * chunk, chunk), chunk)

    def loop(low, high, body):
        def step(i, carry):
            body(i)
            return carry

        lax.fori_loop(low, high, step, 0)

    def dot(a, b):
        return jnp.dot(a, b, preferred_element_type=jnp.float32)

    def dot_rows(a, b):
        return lax.dot_general(a, b, (((0,), (0,)), ((), ())), preferred_element_type=jnp.float32)

    def dot_cols(a, b):
        return lax.dot_general(a, b, (((1,), (1,)), ((), ())), preferred_element_type=jnp.float32)

    mine = pl.ds(pl.multiple_of(f * cols, cols), cols)
    weights = [
        pltpu.make_async_copy(w_self.at[:, mine], self_cols, w_sem.at[0]),
        pltpu.make_async_copy(w_neigh.at[:, mine], neigh_cols, w_sem.at[1]),
        pltpu.make_async_copy(w_self.at[mine, :], self_rows, w_sem.at[2]),
        pltpu.make_async_copy(w_neigh.at[mine, :], neigh_rows, w_sem.at[3]),
    ]
    for w in weights:
        w.start()

    barrier = pltpu.get_barrier_semaphore()
    for d in range(1, parts):
        pl.semaphore_signal(barrier, inc=1, device_id=((g + d) % parts, f), device_id_type=MESH)
    for d in range(1, feats):
        pl.semaphore_signal(barrier, inc=1, device_id=(g, (f + d) % feats), device_id_type=MESH)
    pl.semaphore_wait(barrier, parts + feats - 2)

    def id_copy(slot, p):
        return remote(out_ids.at[p], in_ids.at[slot], i_send.at[p], i_recv.at[slot], p, f)

    def block_copy(slot, p):
        return remote(out_blocks.at[p], in_blocks.at[slot], a_send.at[p], a_recv.at[slot], p, f)

    def return_copy(slot, p):
        return remote(back_out.at[p], back_in.at[slot], r_send.at[p], r_recv.at[slot], p, f)

    def send_blocks(d):
        p = (g + d) % parts
        id_copy(g, p).start()
        block_copy(g, p).start()

    loop(1, parts, send_blocks)

    def to_sibling(n, full, c):
        piece = full.at[f, span(c)]
        return remote(piece, piece, gs_send.at[n, c], g_recv.at[n, f, c], g, sibling)

    def to_chip(n, full, c, d):
        piece = full.at[f, span(c)]
        return remote(piece, piece, gx_send.at[n, d - 1, c], g_recv.at[n, f, c], g, (x + d) % chips * 2 + core)

    def relay(n, full, c, d):
        j = (x + d) % chips * 2 + core
        piece = full.at[j, span(c)]
        return remote(piece, piece, gr_send.at[n, d - 1, c], g_recv.at[n, j, c], g, sibling)

    def arrival(n, full, c, j):
        piece = full.at[j, span(c)]
        return remote(piece, piece, gs_send.at[n, c], g_recv.at[n, j, c], g, sibling)

    def gather_start(n, full, c):
        for d in range(1, chips):
            to_chip(n, full, c, d).start()
        to_sibling(n, full, c).start()

    def gather_relay(n, full, c):
        for d in range(1, chips):
            arrival(n, full, c, (x + d) % chips * 2 + core).wait_recv()
            relay(n, full, c, d).start()

    def gather_finish(n, full, c):
        arrival(n, full, c, sibling).wait_recv()
        for d in range(1, chips):
            arrival(n, full, c, (x + d) % chips * 2 + 1 - core).wait_recv()

    def gather_sent(n, full, c):
        to_sibling(n, full, c).wait_send()
        for d in range(1, chips):
            to_chip(n, full, c, d).wait_send()
            relay(n, full, c, d).wait_send()

    def feat_start(c):
        feat_full[f, span(c), :] = feat_ref[span(c), :]
        gather_start(0, feat_full, c)

    loop(0, CHUNKS, feat_start)

    cap = out_blocks.shape[1]

    def scatter(ids, values, first):
        def tile(c):
            node = lax.broadcasted_iota(jnp.int32, (chunk, cap), 0) + c * chunk
            match = jnp.where(node == ids, 1.0, 0.0).astype(jnp.bfloat16)
            added = dot(match, values)
            if first:
                sum_ref[span(c), :] = added
            else:
                sum_ref[span(c), :] += added

        loop(0, CHUNKS, tile)

    scatter(out_ids[g][0:1, :], out_blocks[g], True)
    in_ids[g] = out_ids[g]

    def take_blocks(d):
        p = (g + parts - d) % parts
        id_copy(p, p).wait_recv()
        block_copy(p, p).wait_recv()
        scatter(in_ids[p][0:1, :], in_blocks[p], False)

    loop(1, parts, take_blocks)

    def aggregate(c):
        agg_full[f, span(c), :] = (sum_ref[span(c), :] / deg_ref[span(c), :]).astype(jnp.bfloat16)
        gather_start(1, agg_full, c)

    loop(0, CHUNKS, aggregate)
    loop(0, CHUNKS, lambda c: gather_relay(0, feat_full, c))
    for w in weights:
        w.wait()

    def own_term(c):
        gather_finish(0, feat_full, c)
        total = dot(feat_full[0, span(c), :], self_cols[0:cols, :])
        for j in range(1, feats):
            total += dot(feat_full[j, span(c), :], self_cols[j * cols:(j + 1) * cols, :])
        pre_ref[span(c), :] = total

    loop(0, CHUNKS, own_term)

    def activate(c):
        gather_relay(1, agg_full, c)
        gather_finish(1, agg_full, c)
        total = pre_ref[span(c), :]
        for j in range(feats):
            total += dot(agg_full[j, span(c), :], neigh_cols[j * cols:(j + 1) * cols, :])
        sig = jax.nn.sigmoid(total)
        hidden_ref[span(c), :] = (total * sig).astype(jnp.bfloat16)
        slope = sig * (1.0 + total * (1.0 - sig))
        grad_full[f, span(c), :] = (cot_ref[span(c), :].astype(jnp.float32) * slope).astype(jnp.bfloat16)
        gather_start(2, grad_full, c)

    loop(0, CHUNKS, activate)

    def weight_grads(c):
        for j in range(feats):
            at = slice(j * cols, (j + 1) * cols)
            weight_acc[0:cols, at] += dot_rows(feat_ref[span(c), :], grad_full[j, span(c), :])
            weight_acc[cols:2 * cols, at] += dot_rows(agg_full[f, span(c), :], grad_full[j, span(c), :])

    def back_rows(c):
        gather_relay(2, grad_full, c)
        gather_finish(2, grad_full, c)
        total = dot_cols(grad_full[0, span(c), :], neigh_rows[:, 0:cols])
        for j in range(1, feats):
            total += dot_cols(grad_full[j, span(c), :], neigh_rows[:, j * cols:(j + 1) * cols])
        back_ref[span(c), :] = (total / deg_ref[span(c), :]).astype(jnp.bfloat16)

    weight_acc[...] = jnp.zeros_like(weight_acc)

    def backward(c):
        back_rows(c)
        weight_grads(c)

    loop(0, CHUNKS - 1, backward)
    back_rows(CHUNKS - 1)

    def pick(p):
        ids = jnp.transpose(in_ids[p])[:, 0:1]
        total = jnp.zeros((cap, cols), jnp.float32)
        for c in range(CHUNKS):
            node = lax.broadcasted_iota(jnp.int32, (cap, chunk), 1) + c * chunk
            match = jnp.where(node == ids, 1.0, 0.0).astype(jnp.bfloat16)
            total += dot(match, back_ref[c * chunk:(c + 1) * chunk, :])
        return total.astype(jnp.bfloat16)

    def send_back(d):
        p = (g + d) % parts
        back_out[p] = pick(p)
        return_copy(g, p).start()

    loop(1, parts, send_back)
    back_in[g] = pick(g)
    weight_grads(CHUNKS - 1)

    tall, wide = 2 * cols // ys, width // zs
    for a in range(ys):
        for b in range(zs):
            y_out[a, b] = weight_acc[a * tall:(a + 1) * tall, b * wide:(b + 1) * wide].astype(jnp.bfloat16)

    def y_copy(slot, to):
        return remote(y_out.at[to], y_in.at[slot], ys_send.at[to], ys_recv.at[slot], z * ys + to, f)

    def z_copy(slot, to):
        return remote(z_out.at[to], z_in.at[slot], zs_send.at[to], zs_recv.at[slot], to * ys + y, f)

    def z_gather(slot, to):
        return remote(z_all.at[slot], z_all.at[slot], za_send.at[to], za_recv.at[slot], to * ys + y, f)

    def y_gather(slot, to):
        return remote(y_all.at[slot], y_all.at[slot], ya_send.at[to], ya_recv.at[slot], z * ys + to, f)

    for d in range(1, ys):
        y_copy(y, (y + d) % ys).start()

    def self_part(c):
        total = dot_cols(grad_full[0, span(c), :], self_rows[:, 0:cols])
        for j in range(1, feats):
            total += dot_cols(grad_full[j, span(c), :], self_rows[:, j * cols:(j + 1) * cols])
        self_grad_ref[span(c), :] = total

    loop(0, CHUNKS, self_part)
    y_in[y] = y_out[y]
    for d in range(1, ys):
        p = (y + d) % ys
        y_copy(p, p).wait_recv()
    for b in range(zs):
        total = y_in[0, b].astype(jnp.float32)
        for a in range(1, ys):
            total += y_in[a, b].astype(jnp.float32)
        z_out[b] = total.astype(jnp.bfloat16)
    for d in range(1, zs):
        z_copy(z, (z + d) % zs).start()
    z_in[z] = z_out[z]
    for d in range(1, zs):
        p = (z + d) % zs
        z_copy(p, p).wait_recv()
    total = z_in[0].astype(jnp.float32)
    for b in range(1, zs):
        total += z_in[b].astype(jnp.float32)
    z_all[z] = total.astype(jnp.bfloat16)
    for d in range(1, zs):
        z_gather(z, (z + d) % zs).start()
    for d in range(1, zs):
        p = (z + d) % zs
        z_gather(p, p).wait_recv()
    y_all[y] = z_all[...]
    for d in range(1, ys):
        y_gather(y, (y + d) % ys).start()

    def returned(d):
        p = (g + parts - d) % parts
        return_copy(p, p).wait_recv()
        returned_ref[p] = back_in[p]

    returned_ref[g] = back_in[g]
    loop(1, parts, returned)

    for d in range(1, ys):
        p = (y + d) % ys
        y_gather(p, p).wait_recv()
    for a in range(ys):
        for b in range(zs):
            piece = y_all[a, b].astype(jnp.float32)
            at = slice(b * wide, (b + 1) * wide)
            if a < ys // 2:
                grad_self_ref[a * tall:(a + 1) * tall, at] = piece
            else:
                low = a - ys // 2
                grad_neigh_ref[low * tall:(low + 1) * tall, at] = piece

    def sent(d):
        p = (g + d) % parts
        id_copy(g, p).wait_send()
        block_copy(g, p).wait_send()
        return_copy(g, p).wait_send()

    loop(1, parts, sent)
    for n, full in enumerate((feat_full, agg_full, grad_full)):
        loop(0, CHUNKS, functools.partial(gather_sent, n, full))
    for d in range(1, ys):
        y_copy(y, (y + d) % ys).wait_send()
        y_gather(y, (y + d) % ys).wait_send()
    for d in range(1, zs):
        z_copy(z, (z + d) % zs).wait_send()
        z_gather(z, (z + d) % zs).wait_send()


def layer(outgoing, row_ids, features, degrees, cotangent, w_self, w_neigh):
    parts, cap, cols = outgoing.shape
    nodes = features.shape[0]
    feats = lax.axis_size("feat")
    width = feats * cols
    ys = feats // 2
    zs = parts // ys
    tall, wide = 2 * cols // ys, width // zs
    bf16, f32 = jnp.bfloat16, jnp.float32
    dma = pltpu.SemaphoreType.DMA
    hops = max(feats // 2 - 1, 1)
    return pl.pallas_call(
        functools.partial(layer_kernel, parts, feats),
        out_shape=(
            jax.ShapeDtypeStruct((nodes, cols), bf16),
            jax.ShapeDtypeStruct((parts, cap, cols), bf16),
            jax.ShapeDtypeStruct((nodes, cols), f32),
            jax.ShapeDtypeStruct((cols, width), f32),
            jax.ShapeDtypeStruct((cols, width), f32),
        ),
        in_specs=[pl.BlockSpec(memory_space=VMEM)] * 5 + [pl.BlockSpec(memory_space=pl.ANY)] * 2,
        out_specs=[pl.BlockSpec(memory_space=VMEM)] * 5,
        scratch_shapes=[
            pltpu.VMEM((parts, cap, cols), bf16),
            pltpu.VMEM(row_ids.shape, jnp.int32),
            pltpu.VMEM((nodes, cols), f32),
            pltpu.VMEM((nodes, cols), f32),
            pltpu.VMEM((feats, nodes, cols), bf16),
            pltpu.VMEM((feats, nodes, cols), bf16),
            pltpu.VMEM((feats, nodes, cols), bf16),
            pltpu.VMEM((nodes, cols), bf16),
            pltpu.VMEM((parts, cap, cols), bf16),
            pltpu.VMEM((parts, cap, cols), bf16),
            pltpu.VMEM((width, cols), bf16),
            pltpu.VMEM((width, cols), bf16),
            pltpu.VMEM((cols, width), bf16),
            pltpu.VMEM((cols, width), bf16),
            pltpu.VMEM((2 * cols, width), f32),
            pltpu.VMEM((ys, zs, tall, wide), bf16),
            pltpu.VMEM((ys, zs, tall, wide), bf16),
            pltpu.VMEM((zs, tall, wide), bf16),
            pltpu.VMEM((zs, tall, wide), bf16),
            pltpu.VMEM((zs, tall, wide), bf16),
            pltpu.VMEM((ys, zs, tall, wide), bf16),
            dma((parts,)), dma((parts,)), dma((parts,)), dma((parts,)), dma((parts,)), dma((parts,)),
            dma((4,)),
            dma((3, hops, CHUNKS)), dma((3, CHUNKS)), dma((3, hops, CHUNKS)), dma((3, feats, CHUNKS)),
            dma((ys,)), dma((ys,)), dma((zs,)), dma((zs,)), dma((zs,)), dma((zs,)), dma((ys,)), dma((ys,)),
        ],
        compiler_params=pltpu.CompilerParams(
            collective_id=0, has_side_effects=True, vmem_limit_bytes=56 * 2**20
        ),
        name="layer",
    )(outgoing, row_ids, features, degrees, cotangent, w_self, w_neigh)


def on_device(
    features,
    w_self,
    w_neigh,
    adjacency,
    block_source,
    block_to_slot,
    send_rows,
    send_counts,
    degree,
    cotangent,
):
    part_count = lax.axis_size("graph")
    feat_cols = features.shape[1]
    block_size = adjacency.shape[1]
    slot_cap = send_rows.shape[2]
    slot_total = part_count * slot_cap // block_size
    outgoing = collect(block_source, block_to_slot, send_counts, adjacency, features, slot_total)
    is_live = jnp.arange(slot_cap, dtype=jnp.int32)[None, :] < send_counts[0][:, None]
    row_ids = jnp.where(is_live, send_rows[0], -1)
    row_ids = jnp.broadcast_to(row_ids[:, None, :], (part_count, 8, slot_cap))
    degrees = degree.astype(jnp.float32)[:, None]
    hidden_out, returned, self_grad, grad_self, grad_neigh = layer(
        outgoing.reshape(part_count, slot_cap, feat_cols), row_ids, features, degrees, cotangent, w_self, w_neigh
    )
    grad_features = spread(
        block_source, block_to_slot, adjacency,
        returned.reshape(slot_total, block_size, feat_cols), self_grad,
    )
    return (hidden_out, grad_features, grad_self, grad_neigh)


def solution(mesh):
    placed = (
        P("graph", "feat"),
        P(),
        P(),
        P("graph", None, None),
        P("graph"),
        P("graph"),
        P("graph", None, None),
        P("graph", None),
        P("graph"),
        P("graph", "feat"),
    )
    return jax.shard_map(
        on_device,
        mesh=mesh,
        in_specs=placed,
        out_specs=(P("graph", "feat"), P("graph", "feat"), P("feat", None), P("feat", None)),
        check_vma=False,
    )
```

```python
import functools

import jax
import jax.numpy as jnp
from jax import lax
from jax.experimental import pallas as pl
from jax.experimental.pallas import tpu as pltpu
from jax.sharding import PartitionSpec as P

SMEM = pltpu.SMEM
VMEM = pltpu.VMEM
MESH = pl.DeviceIdType.MESH
GROUP = 4
CHUNKS = 4


def collect_kernel(source_ref, slot_ref, count_ref, adj_hbm, feat_hbm, out_ref, acc, adj_ref, feat_ref, sems):
    adj_copy = pltpu.make_async_copy(adj_hbm, adj_ref, sems.at[0])
    feat_copy = pltpu.make_async_copy(feat_hbm, feat_ref, sems.at[1])
    adj_copy.start()
    feat_copy.start()
    blocks, block, _ = adj_ref.shape
    slot_total = out_ref.shape[0]
    halves = slot_total // count_ref.shape[1]
    acc[...] = jnp.zeros_like(acc)
    adj_copy.wait()
    feat_copy.wait()

    def add(step, carry):
        prods = []
        for j in range(GROUP):
            k = step * GROUP + j
            rows = pl.ds(pl.multiple_of(source_ref[k] * block, block), block)
            prods.append(jnp.dot(adj_ref[k], feat_ref[rows, :], preferred_element_type=jnp.float32))
        for j in range(GROUP):
            acc[slot_ref[step * GROUP + j]] += prods[j]
        return carry

    lax.fori_loop(0, blocks // GROUP, add, 0)

    def finish(s, carry):
        limit = count_ref[0, s // halves] - (s % halves) * block
        rows = lax.broadcasted_iota(jnp.int32, out_ref.shape[1:], 0)
        out_ref[s] = jnp.where(rows < limit, acc[s], 0.0).astype(jnp.bfloat16)
        return carry

    lax.fori_loop(0, slot_total, finish, 0)


def collect(block_source, block_to_slot, send_counts, adjacency, features, slot_total):
    blocks, block, _ = adjacency.shape
    shape = (slot_total, block, features.shape[1])
    return pl.pallas_call(
        collect_kernel,
        out_shape=jax.ShapeDtypeStruct(shape, jnp.bfloat16),
        in_specs=[pl.BlockSpec(memory_space=SMEM)] * 3 + [pl.BlockSpec(memory_space=pl.ANY)] * 2,
        out_specs=pl.BlockSpec(memory_space=VMEM),
        scratch_shapes=[
            pltpu.VMEM(shape, jnp.float32),
            pltpu.VMEM(adjacency.shape, jnp.bfloat16),
            pltpu.VMEM(features.shape, jnp.bfloat16),
            pltpu.SemaphoreType.DMA((2,)),
        ],
        compiler_params=pltpu.CompilerParams(vmem_limit_bytes=32 * 2**20),
        name="collect",
    )(block_source, block_to_slot, send_counts, adjacency, features)


def spread_kernel(
    source_ref, slot_ref, adj_hbm, ret_hbm, start_hbm, hidden_in, self_in, neigh_in,
    out_ref, hidden_out, self_out, neigh_out, acc, adj_ref, ret_ref, sems,
):
    loads = [
        pltpu.make_async_copy(adj_hbm, adj_ref, sems.at[0]),
        pltpu.make_async_copy(ret_hbm, ret_ref, sems.at[1]),
        pltpu.make_async_copy(start_hbm, acc, sems.at[2]),
    ]
    results = [
        pltpu.make_async_copy(hidden_in, hidden_out, sems.at[3]),
        pltpu.make_async_copy(self_in, self_out, sems.at[4]),
        pltpu.make_async_copy(neigh_in, neigh_out, sems.at[5]),
    ]
    for copy in loads + results:
        copy.start()
    for copy in loads:
        copy.wait()
    blocks, block, _ = adj_ref.shape
    sources = out_ref.shape[0] // block

    def add(step, carry):
        prods = []
        for j in range(GROUP):
            k = step * GROUP + j
            prods.append(lax.dot_general(
                adj_ref[k], ret_ref[slot_ref[k]], (((0,), (0,)), ((), ())),
                preferred_element_type=jnp.float32,
            ))
        for j in range(GROUP):
            acc[source_ref[step * GROUP + j]] += prods[j]
        return carry

    lax.fori_loop(0, blocks // GROUP, add, 0)

    def finish(b, carry):
        rows = pl.ds(pl.multiple_of(b * block, block), block)
        out_ref[rows, :] = acc[b].astype(jnp.bfloat16)
        return carry

    lax.fori_loop(0, sources, finish, 0)
    for copy in results:
        copy.wait()


def spread(block_source, block_to_slot, adjacency, returned, self_grad, hidden, grad_self, grad_neigh):
    blocks, block, _ = adjacency.shape
    nodes, cols = self_grad.shape
    shape = (nodes // block, block, cols)
    passed = [jax.ShapeDtypeStruct(v.shape, v.dtype) for v in (hidden, grad_self, grad_neigh)]
    return pl.pallas_call(
        spread_kernel,
        out_shape=[jax.ShapeDtypeStruct((nodes, cols), jnp.bfloat16)] + passed,
        in_specs=[pl.BlockSpec(memory_space=SMEM)] * 2 + [pl.BlockSpec(memory_space=pl.ANY)] * 6,
        out_specs=[pl.BlockSpec(memory_space=VMEM)] + [pl.BlockSpec(memory_space=pl.ANY)] * 3,
        scratch_shapes=[
            pltpu.VMEM(shape, jnp.float32),
            pltpu.VMEM(adjacency.shape, jnp.bfloat16),
            pltpu.VMEM(returned.shape, jnp.bfloat16),
            pltpu.SemaphoreType.DMA((6,)),
        ],
        compiler_params=pltpu.CompilerParams(vmem_limit_bytes=32 * 2**20),
        name="spread",
    )(block_source, block_to_slot, adjacency, returned, self_grad.reshape(shape), hidden, grad_self, grad_neigh)


def layer_kernel(
    parts, feats,
    count_ref, out_blocks, rows_ref, degree_ref, feat_hbm, cot_hbm, w_self, w_neigh,
    hidden_ref, returned_ref, self_grad_ref, grad_self_ref, grad_neigh_ref,
    out_ids, deg_ref, cot_ref, in_blocks, in_ids, sum_ref, pre_ref, feat_full, agg_full, grad_full, back_ref, back_out, back_in,
    self_cols, neigh_cols, self_rows, neigh_rows, weight_acc,
    y_out, y_in, z_out, z_in, z_all, y_all,
    a_send, a_recv, i_send, i_recv, r_send, r_recv, w_sem, f_sem,
    gx_send, gs_send, gr_send, g_recv,
    ys_send, ys_recv, zs_send, zs_recv, za_send, za_recv, ya_send, ya_recv,
):
    g, f = lax.axis_index("graph"), lax.axis_index("feat")
    chips = feats // 2
    ys = chips
    zs = parts // ys
    x, core = f // 2, f % 2
    sibling = x * 2 + 1 - core
    z, y = g // ys, g % ys
    nodes, cols = feat_hbm.shape
    cap = out_blocks.shape[1]
    width = feats * cols
    chunk = nodes // CHUNKS

    def remote(src, dst, send, recv, graph_to, feat_to):
        return pltpu.make_async_remote_copy(
            src_ref=src, dst_ref=dst, send_sem=send, recv_sem=recv,
            device_id=(graph_to, feat_to), device_id_type=MESH,
        )

    def span(c):
        return pl.ds(pl.multiple_of(c * chunk, chunk), chunk)

    def loop(low, high, body):
        def step(i, carry):
            body(i)
            return carry

        lax.fori_loop(low, high, step, 0)

    def dot(a, b):
        return jnp.dot(a, b, preferred_element_type=jnp.float32)

    def dot_rows(a, b):
        return lax.dot_general(a, b, (((0,), (0,)), ((), ())), preferred_element_type=jnp.float32)

    def dot_cols(a, b):
        return lax.dot_general(a, b, (((1,), (1,)), ((), ())), preferred_element_type=jnp.float32)

    mine = pl.ds(pl.multiple_of(f * cols, cols), cols)
    weights = [
        pltpu.make_async_copy(w_self.at[:, mine], self_cols, w_sem.at[0]),
        pltpu.make_async_copy(w_neigh.at[:, mine], neigh_cols, w_sem.at[1]),
        pltpu.make_async_copy(w_self.at[mine, :], self_rows, w_sem.at[2]),
        pltpu.make_async_copy(w_neigh.at[mine, :], neigh_rows, w_sem.at[3]),
        pltpu.make_async_copy(cot_hbm, cot_ref, w_sem.at[4]),
    ]

    def feat_copy(c):
        return pltpu.make_async_copy(feat_hbm.at[span(c)], feat_full.at[f, span(c)], f_sem.at[c])

    loop(0, CHUNKS, lambda c: feat_copy(c).start())
    for w in weights:
        w.start()
    for p in range(parts):
        lane = lax.broadcasted_iota(jnp.int32, (8, cap), 1)
        ids = jnp.broadcast_to(rows_ref[0, p:p + 1, :], (8, cap))
        out_ids[p] = jnp.where(lane < count_ref[0, p], ids, -1)

    barrier = pltpu.get_barrier_semaphore()
    for d in range(1, parts):
        pl.semaphore_signal(barrier, inc=1, device_id=((g + d) % parts, f), device_id_type=MESH)
    for d in range(1, feats):
        pl.semaphore_signal(barrier, inc=1, device_id=(g, (f + d) % feats), device_id_type=MESH)
    pl.semaphore_wait(barrier, parts + feats - 2)

    def id_copy(slot, p):
        return remote(out_ids.at[p], in_ids.at[slot], i_send.at[p], i_recv.at[slot], p, f)

    def block_copy(slot, p):
        return remote(out_blocks.at[p], in_blocks.at[slot], a_send.at[p], a_recv.at[slot], p, f)

    def return_copy(slot, p):
        return remote(back_out.at[p], back_in.at[slot], r_send.at[p], r_recv.at[slot], p, f)

    def send_blocks(d):
        p = (g + d) % parts
        id_copy(g, p).start()
        block_copy(g, p).start()

    loop(1, parts, send_blocks)

    def to_sibling(n, full, c):
        piece = full.at[f, span(c)]
        return remote(piece, piece, gs_send.at[n, c], g_recv.at[n, f, c], g, sibling)

    def to_chip(n, full, c, d):
        piece = full.at[f, span(c)]
        return remote(piece, piece, gx_send.at[n, d - 1, c], g_recv.at[n, f, c], g, (x + d) % chips * 2 + core)

    def relay(n, full, c, d):
        j = (x + d) % chips * 2 + core
        piece = full.at[j, span(c)]
        return remote(piece, piece, gr_send.at[n, d - 1, c], g_recv.at[n, j, c], g, sibling)

    def arrival(n, full, c, j):
        piece = full.at[j, span(c)]
        return remote(piece, piece, gs_send.at[n, c], g_recv.at[n, j, c], g, sibling)

    def gather_start(n, full, c):
        for d in range(1, chips):
            to_chip(n, full, c, d).start()
        to_sibling(n, full, c).start()

    def gather_relay(n, full, c):
        for d in range(1, chips):
            arrival(n, full, c, (x + d) % chips * 2 + core).wait_recv()
            relay(n, full, c, d).start()

    def gather_finish(n, full, c):
        arrival(n, full, c, sibling).wait_recv()
        gather_relayed(n, full, c)

    def gather_relayed(n, full, c):
        for d in range(1, chips):
            arrival(n, full, c, (x + d) % chips * 2 + 1 - core).wait_recv()

    def gather_sent(n, full, c):
        to_sibling(n, full, c).wait_send()
        for d in range(1, chips):
            to_chip(n, full, c, d).wait_send()
            relay(n, full, c, d).wait_send()

    def feat_start(c):
        feat_copy(c).wait()
        gather_start(0, feat_full, c)

    loop(0, CHUNKS, feat_start)
    columns = jnp.transpose(degree_ref[...].astype(jnp.float32))
    lanes = degree_ref.shape[1]
    for b in range(nodes // lanes):
        deg_ref[b * lanes:(b + 1) * lanes, :] = jnp.broadcast_to(columns[:, b:b + 1], (lanes, 128))

    def scatter(ids, values, first):
        def tile(c):
            node = lax.broadcasted_iota(jnp.int32, (chunk, cap), 0) + c * chunk
            match = jnp.where(node == ids, 1.0, 0.0).astype(jnp.bfloat16)
            added = dot(match, values)
            if first:
                sum_ref[span(c), :] = added
            else:
                sum_ref[span(c), :] += added

        loop(0, CHUNKS, tile)

    scatter(out_ids[g][0:1, :], out_blocks[g], True)
    in_ids[g] = out_ids[g]

    def take_blocks(d):
        p = (g + parts - d) % parts
        id_copy(p, p).wait_recv()
        block_copy(p, p).wait_recv()
        scatter(in_ids[p][0:1, :], in_blocks[p], False)

    loop(1, parts, take_blocks)

    def aggregate(c):
        agg_full[f, span(c), :] = (sum_ref[span(c), :] / deg_ref[span(c), 0:1]).astype(jnp.bfloat16)
        gather_start(1, agg_full, c)

    loop(0, CHUNKS, aggregate)
    loop(0, CHUNKS, lambda c: gather_relay(0, feat_full, c))
    for w in weights:
        w.wait()

    def own_term(c):
        gather_finish(0, feat_full, c)
        total = dot(feat_full[0, span(c), :], self_cols[0:cols, :])
        for j in range(1, feats):
            total += dot(feat_full[j, span(c), :], self_cols[j * cols:(j + 1) * cols, :])
        pre_ref[span(c), :] = total

    loop(0, CHUNKS, own_term)

    def activate(c):
        gather_relay(1, agg_full, c)
        gather_finish(1, agg_full, c)
        total = pre_ref[span(c), :]
        for j in range(feats):
            total += dot(agg_full[j, span(c), :], neigh_cols[j * cols:(j + 1) * cols, :])
        sig = jax.nn.sigmoid(total)
        hidden_ref[span(c), :] = (total * sig).astype(jnp.bfloat16)
        slope = sig * (1.0 + total * (1.0 - sig))
        grad_full[f, span(c), :] = (cot_ref[span(c), :].astype(jnp.float32) * slope).astype(jnp.bfloat16)
        gather_start(2, grad_full, c)

    loop(0, CHUNKS, activate)

    def weight_grads(d, c):
        q = (x + d) % chips
        for k in range(2):
            at = slice(k * cols, (k + 1) * cols)
            right = grad_full[q * 2 + k, span(c), :]
            weight_acc[d, 0:cols, at] += dot_rows(feat_full[f, span(c), :], right)
            weight_acc[d, cols:2 * cols, at] += dot_rows(agg_full[f, span(c), :], right)

    def back_rows(c):
        gather_relay(2, grad_full, c)
        gather_relayed(2, grad_full, c)
        total = dot_cols(grad_full[0, span(c), :], neigh_rows[:, 0:cols])
        for j in range(1, feats):
            total += dot_cols(grad_full[j, span(c), :], neigh_rows[:, j * cols:(j + 1) * cols])
        back_ref[span(c), :] = (total / deg_ref[span(c), 0:1]).astype(jnp.bfloat16)

    weight_acc[...] = jnp.zeros_like(weight_acc)

    tall = 2 * cols // parts

    def pieces():
        return [(a, b, (a * zs + b) * tall) for a in range(ys) for b in range(zs)]

    def y_copy(n, slot, to):
        return remote(y_out.at[n, to], y_in.at[n, slot], ys_send.at[n, to], ys_recv.at[n, slot], z * ys + to, f)

    def z_copy(n, slot, to):
        return remote(z_out.at[n, to], z_in.at[n, slot], zs_send.at[n, to], zs_recv.at[n, slot], to * ys + y, f)

    def z_gather(n, slot, to):
        piece = z_all.at[n, slot]
        return remote(piece, piece, za_send.at[n, to], za_recv.at[n, slot], to * ys + y, f)

    def y_gather(n, slot, to):
        piece = y_all.at[n, slot]
        return remote(piece, piece, ya_send.at[n, to], ya_recv.at[n, slot], z * ys + to, f)

    def reduce_start(n):
        for a, b, row in pieces():
            y_out[n, a, b] = weight_acc[n, row:row + tall, :].astype(jnp.bfloat16)
        for d in range(1, ys):
            y_copy(n, y, (y + d) % ys).start()
        y_in[n, y] = y_out[n, y]

    def reduce_z(n):
        for d in range(1, ys):
            p = (y + d) % ys
            y_copy(n, p, p).wait_recv()
        for b in range(zs):
            total = y_in[n, 0, b].astype(jnp.float32)
            for a in range(1, ys):
                total += y_in[n, a, b].astype(jnp.float32)
            z_out[n, b] = total.astype(jnp.bfloat16)
        for d in range(1, zs):
            z_copy(n, z, (z + d) % zs).start()
        z_in[n, z] = z_out[n, z]

    def finish_z(n):
        for d in range(1, zs):
            p = (z + d) % zs
            z_copy(n, p, p).wait_recv()
        total = z_in[n, 0].astype(jnp.float32)
        for b in range(1, zs):
            total += z_in[n, b].astype(jnp.float32)
        z_all[n, z] = total.astype(jnp.bfloat16)
        for d in range(1, zs):
            z_gather(n, z, (z + d) % zs).start()

    def finish_y(n):
        for d in range(1, zs):
            p = (z + d) % zs
            z_gather(n, p, p).wait_recv()
        y_all[n, y] = z_all[n]
        for d in range(1, ys):
            y_gather(n, y, (y + d) % ys).start()

    def write_grads(n):
        for d in range(1, ys):
            p = (y + d) % ys
            y_gather(n, p, p).wait_recv()
        at = pl.ds(pl.multiple_of((x + n) % chips * 2 * cols, 2 * cols), 2 * cols)
        for a, b, row in pieces():
            piece = y_all[n, a, b].astype(jnp.float32)
            if row < cols:
                grad_self_ref[row:row + tall, at] = piece
            else:
                grad_neigh_ref[row - cols:row - cols + tall, at] = piece

    def sibling_grads(c):
        arrival(2, grad_full, c, sibling).wait_recv()
        weight_grads(0, c)

    stages = (reduce_z, finish_z, finish_y)
    others = range(1, chips)
    loop(0, CHUNKS, sibling_grads)
    reduce_start(0)
    for c in range(CHUNKS):
        back_rows(c)
        for d in others:
            weight_grads(d, c)
        if c < len(stages):
            stages[c](0)

    def pick(p):
        ids = jnp.transpose(in_ids[p])[:, 0:1]
        total = jnp.zeros((cap, cols), jnp.float32)
        for c in range(CHUNKS):
            node = lax.broadcasted_iota(jnp.int32, (cap, chunk), 1) + c * chunk
            match = jnp.where(node == ids, 1.0, 0.0).astype(jnp.bfloat16)
            total += dot(match, back_ref[c * chunk:(c + 1) * chunk, :])
        return total.astype(jnp.bfloat16)

    def send_back(d):
        p = (g + d) % parts
        back_out[p] = pick(p)
        return_copy(g, p).start()

    for n in others:
        reduce_start(n)
    loop(1, parts // 2, send_back)
    for n in others:
        reduce_z(n)
    loop(parts // 2, parts, send_back)
    back_in[g] = pick(g)
    returned_ref[g] = back_in[g]
    for n in others:
        finish_z(n)

    def self_part(c):
        total = dot_cols(grad_full[0, span(c), :], self_rows[:, 0:cols])
        for j in range(1, feats):
            total += dot_cols(grad_full[j, span(c), :], self_rows[:, j * cols:(j + 1) * cols])
        self_grad_ref[span(c), :] = total

    loop(0, CHUNKS, self_part)
    write_grads(0)
    for n in others:
        finish_y(n)

    def returned(d):
        p = (g + parts - d) % parts
        return_copy(p, p).wait_recv()
        returned_ref[p] = back_in[p]

    loop(1, parts, returned)
    for n in others:
        write_grads(n)

    def sent(d):
        p = (g + d) % parts
        id_copy(g, p).wait_send()
        block_copy(g, p).wait_send()
        return_copy(g, p).wait_send()

    loop(1, parts, sent)
    for n, full in enumerate((feat_full, agg_full, grad_full)):
        loop(0, CHUNKS, functools.partial(gather_sent, n, full))
    for n in range(chips):
        for d in range(1, ys):
            y_copy(n, y, (y + d) % ys).wait_send()
            y_gather(n, y, (y + d) % ys).wait_send()
        for d in range(1, zs):
            z_copy(n, z, (z + d) % zs).wait_send()
            z_gather(n, z, (z + d) % zs).wait_send()


def layer(send_counts, outgoing, send_rows, degrees, features, cotangent, w_self, w_neigh):
    parts, cap, cols = outgoing.shape
    nodes = features.shape[0]
    feats = lax.axis_size("feat")
    width = feats * cols
    ys = feats // 2
    zs = parts // ys
    chips = feats // 2
    tall, wide = 2 * cols // parts, 2 * cols
    bf16, f32 = jnp.bfloat16, jnp.float32
    dma = pltpu.SemaphoreType.DMA
    hops = max(feats // 2 - 1, 1)
    return pl.pallas_call(
        functools.partial(layer_kernel, parts, feats),
        out_shape=(
            jax.ShapeDtypeStruct((nodes, cols), bf16),
            jax.ShapeDtypeStruct((parts, cap, cols), bf16),
            jax.ShapeDtypeStruct((nodes, cols), f32),
            jax.ShapeDtypeStruct((cols, width), f32),
            jax.ShapeDtypeStruct((cols, width), f32),
        ),
        in_specs=[pl.BlockSpec(memory_space=SMEM)]
        + [pl.BlockSpec(memory_space=VMEM)] * 3
        + [pl.BlockSpec(memory_space=pl.ANY)] * 4,
        out_specs=[pl.BlockSpec(memory_space=VMEM)] * 5,
        scratch_shapes=[
            pltpu.VMEM((parts, 8, cap), jnp.int32),
            pltpu.VMEM((nodes, 128), f32),
            pltpu.VMEM((nodes, cols), bf16),
            pltpu.VMEM((parts, cap, cols), bf16),
            pltpu.VMEM((parts, 8, cap), jnp.int32),
            pltpu.VMEM((nodes, cols), f32),
            pltpu.VMEM((nodes, cols), f32),
            pltpu.VMEM((feats, nodes, cols), bf16),
            pltpu.VMEM((feats, nodes, cols), bf16),
            pltpu.VMEM((feats, nodes, cols), bf16),
            pltpu.VMEM((nodes, cols), bf16),
            pltpu.VMEM((parts, cap, cols), bf16),
            pltpu.VMEM((parts, cap, cols), bf16),
            pltpu.VMEM((width, cols), bf16),
            pltpu.VMEM((width, cols), bf16),
            pltpu.VMEM((cols, width), bf16),
            pltpu.VMEM((cols, width), bf16),
            pltpu.VMEM((chips, 2 * cols, wide), f32),
            pltpu.VMEM((chips, ys, zs, tall, wide), bf16),
            pltpu.VMEM((chips, ys, zs, tall, wide), bf16),
            pltpu.VMEM((chips, zs, tall, wide), bf16),
            pltpu.VMEM((chips, zs, tall, wide), bf16),
            pltpu.VMEM((chips, zs, tall, wide), bf16),
            pltpu.VMEM((chips, ys, zs, tall, wide), bf16),
            dma((parts,)), dma((parts,)), dma((parts,)), dma((parts,)), dma((parts,)), dma((parts,)),
            dma((5,)), dma((CHUNKS,)),
            dma((3, hops, CHUNKS)), dma((3, CHUNKS)), dma((3, hops, CHUNKS)), dma((3, feats, CHUNKS)),
            dma((chips, ys)), dma((chips, ys)), dma((chips, zs)), dma((chips, zs)),
            dma((chips, zs)), dma((chips, zs)), dma((chips, ys)), dma((chips, ys)),
        ],
        compiler_params=pltpu.CompilerParams(
            collective_id=0, has_side_effects=True, vmem_limit_bytes=56 * 2**20
        ),
        name="layer",
    )(send_counts, outgoing, send_rows, degrees, features, cotangent, w_self, w_neigh)


def on_device(
    features,
    w_self,
    w_neigh,
    adjacency,
    block_source,
    block_to_slot,
    send_rows,
    send_counts,
    degree,
    cotangent,
):
    part_count = lax.axis_size("graph")
    feat_cols = features.shape[1]
    block_size = adjacency.shape[1]
    slot_cap = send_rows.shape[2]
    slot_total = part_count * slot_cap // block_size
    outgoing = collect(block_source, block_to_slot, send_counts, adjacency, features, slot_total)
    hidden, returned, self_grad, grad_self, grad_neigh = layer(
        send_counts, outgoing.reshape(part_count, slot_cap, feat_cols), send_rows,
        degree.reshape(-1, block_size), features, cotangent, w_self, w_neigh,
    )
    grad_features, hidden_out, grad_self, grad_neigh = spread(
        block_source, block_to_slot, adjacency,
        returned.reshape(slot_total, block_size, feat_cols), self_grad, hidden, grad_self, grad_neigh,
    )
    return (hidden_out, grad_features, grad_self, grad_neigh)


def solution(mesh):
    placed = (
        P("graph", "feat"),
        P(),
        P(),
        P("graph", None, None),
        P("graph"),
        P("graph"),
        P("graph", None, None),
        P("graph", None),
        P("graph"),
        P("graph", "feat"),
    )
    return jax.shard_map(
        on_device,
        mesh=mesh,
        in_specs=placed,
        out_specs=(P("graph", "feat"), P("graph", "feat"), P("feat", None), P("feat", None)),
        check_vma=False,
    )
```

```python
import functools

import jax
import jax.numpy as jnp
from jax import lax
from jax.experimental import pallas as pl
from jax.experimental.pallas import tpu as pltpu
from jax.sharding import PartitionSpec as P

SMEM = pltpu.SMEM
VMEM = pltpu.VMEM
MESH = pl.DeviceIdType.MESH
GROUP = 4
CHUNKS = 4
VMEM_BYTES = 60 * 2**20


def collect_kernel(source_ref, slot_ref, count_ref, adj_hbm, feat_hbm, out_ref, acc, adj_ref, feat_ref, sems):
    adj_copy = pltpu.make_async_copy(adj_hbm, adj_ref, sems.at[0])
    feat_copy = pltpu.make_async_copy(feat_hbm, feat_ref, sems.at[1])
    adj_copy.start()
    feat_copy.start()
    blocks, block, _ = adj_ref.shape
    slot_total = out_ref.shape[0]
    halves = slot_total // count_ref.shape[1]
    acc[...] = jnp.zeros_like(acc)
    adj_copy.wait()
    feat_copy.wait()

    def add(step, carry):
        prods = []
        for j in range(GROUP):
            k = step * GROUP + j
            rows = pl.ds(pl.multiple_of(source_ref[k] * block, block), block)
            prods.append(jnp.dot(adj_ref[k], feat_ref[rows, :], preferred_element_type=jnp.float32))
        for j in range(GROUP):
            acc[slot_ref[step * GROUP + j]] += prods[j]
        return carry

    lax.fori_loop(0, blocks // GROUP, add, 0)

    def finish(s, carry):
        limit = count_ref[0, s // halves] - (s % halves) * block
        rows = lax.broadcasted_iota(jnp.int32, out_ref.shape[1:], 0)
        out_ref[s] = jnp.where(rows < limit, acc[s], 0.0).astype(jnp.bfloat16)
        return carry

    lax.fori_loop(0, slot_total, finish, 0)


def collect(block_source, block_to_slot, send_counts, adjacency, features, slot_total):
    blocks, block, _ = adjacency.shape
    shape = (slot_total, block, features.shape[1])
    return pl.pallas_call(
        collect_kernel,
        out_shape=jax.ShapeDtypeStruct(shape, jnp.bfloat16),
        in_specs=[pl.BlockSpec(memory_space=SMEM)] * 3 + [pl.BlockSpec(memory_space=pl.ANY)] * 2,
        out_specs=pl.BlockSpec(memory_space=VMEM),
        scratch_shapes=[
            pltpu.VMEM(shape, jnp.float32),
            pltpu.VMEM(adjacency.shape, jnp.bfloat16),
            pltpu.VMEM(features.shape, jnp.bfloat16),
            pltpu.SemaphoreType.DMA((2,)),
        ],
        compiler_params=pltpu.CompilerParams(vmem_limit_bytes=VMEM_BYTES),
        name="collect",
    )(block_source, block_to_slot, send_counts, adjacency, features)


def spread_kernel(
    source_ref, slot_ref, adj_hbm, ret_hbm, start_hbm, hidden_in, self_in, neigh_in,
    out_ref, hidden_out, self_out, neigh_out, acc, adj_ref, ret_ref, sems,
):
    loads = [
        pltpu.make_async_copy(adj_hbm, adj_ref, sems.at[0]),
        pltpu.make_async_copy(ret_hbm, ret_ref, sems.at[1]),
        pltpu.make_async_copy(start_hbm, acc, sems.at[2]),
    ]
    results = [
        pltpu.make_async_copy(hidden_in, hidden_out, sems.at[3]),
        pltpu.make_async_copy(self_in, self_out, sems.at[4]),
        pltpu.make_async_copy(neigh_in, neigh_out, sems.at[5]),
    ]
    for copy in loads + results:
        copy.start()
    for copy in loads:
        copy.wait()
    blocks, block, _ = adj_ref.shape
    sources = out_ref.shape[0] // block

    def add(step, carry):
        prods = []
        for j in range(GROUP):
            k = step * GROUP + j
            prods.append(lax.dot_general(
                adj_ref[k], ret_ref[slot_ref[k]], (((0,), (0,)), ((), ())),
                preferred_element_type=jnp.float32,
            ))
        for j in range(GROUP):
            acc[source_ref[step * GROUP + j]] += prods[j]
        return carry

    lax.fori_loop(0, blocks // GROUP, add, 0)

    def finish(b, carry):
        rows = pl.ds(pl.multiple_of(b * block, block), block)
        out_ref[rows, :] = acc[b].astype(jnp.bfloat16)
        return carry

    lax.fori_loop(0, sources, finish, 0)
    for copy in results:
        copy.wait()


def spread(block_source, block_to_slot, adjacency, returned, self_grad, hidden, grad_self, grad_neigh):
    blocks, block, _ = adjacency.shape
    nodes, cols = self_grad.shape
    shape = (nodes // block, block, cols)
    passed = [jax.ShapeDtypeStruct(v.shape, v.dtype) for v in (hidden, grad_self, grad_neigh)]
    return pl.pallas_call(
        spread_kernel,
        out_shape=[jax.ShapeDtypeStruct((nodes, cols), jnp.bfloat16)] + passed,
        in_specs=[pl.BlockSpec(memory_space=SMEM)] * 2 + [pl.BlockSpec(memory_space=pl.ANY)] * 6,
        out_specs=[pl.BlockSpec(memory_space=VMEM)] + [pl.BlockSpec(memory_space=pl.ANY)] * 3,
        scratch_shapes=[
            pltpu.VMEM(shape, jnp.float32),
            pltpu.VMEM(adjacency.shape, jnp.bfloat16),
            pltpu.VMEM(returned.shape, jnp.bfloat16),
            pltpu.SemaphoreType.DMA((6,)),
        ],
        compiler_params=pltpu.CompilerParams(vmem_limit_bytes=VMEM_BYTES),
        name="spread",
    )(block_source, block_to_slot, adjacency, returned, self_grad.reshape(shape), hidden, grad_self, grad_neigh)


def layer_kernel(
    parts, feats,
    count_ref, out_blocks, rows_ref, degree_ref, feat_hbm, cot_hbm, w_self, w_neigh,
    hidden_hbm, returned_hbm, self_grad_hbm, grad_self_ref, grad_neigh_ref,
    out_ids, deg_ref, cot_ref, in_blocks, in_ids, sum_ref, pre_ref, feat_full, agg_full, grad_full, back_ref, back_out, back_in,
    self_cols, neigh_cols, self_rows, neigh_rows, weight_acc,
    self_turned, neigh_turned, left_turned, hidden_ref, self_grad_ref,
    y_out, y_in, z_out, z_in, z_all, y_all,
    a_send, a_recv, i_send, i_recv, r_send, r_recv, w_sem, f_sem, o_sem, b_sem,
    gx_send, gs_send, gr_send, g_recv,
    ys_send, ys_recv, zs_send, zs_recv, za_send, za_recv, ya_send, ya_recv,
):
    g, f = lax.axis_index("graph"), lax.axis_index("feat")
    chips = feats // 2
    ys = chips
    zs = parts // ys
    x, core = f // 2, f % 2
    sibling = x * 2 + 1 - core
    z, y = g // ys, g % ys
    nodes, cols = feat_hbm.shape
    cap = out_blocks.shape[1]
    width = feats * cols
    chunk = nodes // CHUNKS

    def remote(src, dst, send, recv, graph_to, feat_to):
        return pltpu.make_async_remote_copy(
            src_ref=src, dst_ref=dst, send_sem=send, recv_sem=recv,
            device_id=(graph_to, feat_to), device_id_type=MESH,
        )

    def span(c):
        return pl.ds(pl.multiple_of(c * chunk, chunk), chunk)

    def loop(low, high, body):
        def step(i, carry):
            body(i)
            return carry

        lax.fori_loop(low, high, step, 0)

    def dot(a, b):
        return jnp.dot(a, b, preferred_element_type=jnp.float32)

    mine = pl.ds(pl.multiple_of(f * cols, cols), cols)
    weights = [
        pltpu.make_async_copy(w_self.at[:, mine], self_cols, w_sem.at[0]),
        pltpu.make_async_copy(w_neigh.at[:, mine], neigh_cols, w_sem.at[1]),
        pltpu.make_async_copy(w_self.at[mine, :], self_rows, w_sem.at[2]),
        pltpu.make_async_copy(w_neigh.at[mine, :], neigh_rows, w_sem.at[3]),
        pltpu.make_async_copy(cot_hbm, cot_ref, w_sem.at[4]),
    ]

    def feat_copy(c):
        return pltpu.make_async_copy(feat_hbm.at[span(c)], feat_full.at[f, span(c)], f_sem.at[c])

    loop(0, CHUNKS, lambda c: feat_copy(c).start())
    for w in weights:
        w.start()
    for p in range(parts):
        lane = lax.broadcasted_iota(jnp.int32, (8, cap), 1)
        ids = jnp.broadcast_to(rows_ref[0, p:p + 1, :], (8, cap))
        out_ids[p] = jnp.where(lane < count_ref[0, p], ids, -1)

    barrier = pltpu.get_barrier_semaphore()
    for d in range(1, parts):
        pl.semaphore_signal(barrier, inc=1, device_id=((g + d) % parts, f), device_id_type=MESH)
    for d in range(1, feats):
        pl.semaphore_signal(barrier, inc=1, device_id=(g, (f + d) % feats), device_id_type=MESH)
    pl.semaphore_wait(barrier, parts + feats - 2)

    def id_copy(slot, p):
        return remote(out_ids.at[p], in_ids.at[slot], i_send.at[p], i_recv.at[slot], p, f)

    def block_copy(slot, p):
        return remote(out_blocks.at[p], in_blocks.at[slot], a_send.at[p], a_recv.at[slot], p, f)

    def return_copy(slot, p):
        return remote(back_out.at[p], back_in.at[slot], r_send.at[p], r_recv.at[slot], p, f)

    half = parts // 2

    def peer(i):
        far = (1 - g // half) * half + (g + i) % half
        near = g // half * half + (g + i + 1 - half) % half
        return far * (1 - i // half) + near * (i // half)

    def send_blocks(i):
        p = peer(i)
        id_copy(g, p).start()
        block_copy(g, p).start()

    loop(0, parts - 1, send_blocks)

    def to_sibling(n, full, c):
        piece = full.at[f, span(c)]
        return remote(piece, piece, gs_send.at[n, c], g_recv.at[n, f, c], g, sibling)

    def to_chip(n, full, c, d):
        piece = full.at[f, span(c)]
        return remote(piece, piece, gx_send.at[n, d - 1, c], g_recv.at[n, f, c], g, (x + d) % chips * 2 + core)

    def relay(n, full, c, d):
        j = (x + d) % chips * 2 + core
        piece = full.at[j, span(c)]
        return remote(piece, piece, gr_send.at[n, d - 1, c], g_recv.at[n, j, c], g, sibling)

    def arrival(n, full, c, j):
        piece = full.at[j, span(c)]
        return remote(piece, piece, gs_send.at[n, c], g_recv.at[n, j, c], g, sibling)

    def gather_start(n, full, c):
        for d in range(1, chips):
            to_chip(n, full, c, d).start()
        to_sibling(n, full, c).start()

    def gather_relay(n, full, c):
        for d in range(1, chips):
            arrival(n, full, c, (x + d) % chips * 2 + core).wait_recv()
            relay(n, full, c, d).start()

    def gather_finish(n, full, c):
        arrival(n, full, c, sibling).wait_recv()
        gather_relayed(n, full, c)

    def gather_relayed(n, full, c):
        for d in range(1, chips):
            arrival(n, full, c, (x + d) % chips * 2 + 1 - core).wait_recv()

    def gather_sent(n, full, c):
        to_sibling(n, full, c).wait_send()
        for d in range(1, chips):
            to_chip(n, full, c, d).wait_send()
            relay(n, full, c, d).wait_send()

    def feat_start(c):
        feat_copy(c).wait()
        gather_start(0, feat_full, c)

    loop(0, CHUNKS, feat_start)
    columns = jnp.transpose(degree_ref[...].astype(jnp.float32))
    lanes = degree_ref.shape[1]
    for b in range(nodes // lanes):
        deg_ref[b * lanes:(b + 1) * lanes, :] = jnp.broadcast_to(columns[:, b:b + 1], (lanes, 128))

    def scatter(ids, values, first):
        def tile(c):
            node = lax.broadcasted_iota(jnp.int32, (chunk, cap), 0) + c * chunk
            match = jnp.where(node == ids, 1.0, 0.0).astype(jnp.bfloat16)
            added = dot(match, values)
            if first:
                sum_ref[span(c), :] = added
            else:
                sum_ref[span(c), :] += added

        loop(0, CHUNKS, tile)

    scatter(out_ids[g][0:1, :], out_blocks[g], True)
    in_ids[g] = out_ids[g]

    def take_blocks(i):
        p = peer(parts - 2 - i)
        id_copy(p, p).wait_recv()
        block_copy(p, p).wait_recv()
        scatter(in_ids[p][0:1, :], in_blocks[p], False)

    for w in weights:
        w.wait()
    for j in range(feats):
        at = slice(j * cols, (j + 1) * cols)
        self_turned[at, :] = jnp.transpose(self_rows[:, at])
        neigh_turned[at, :] = jnp.transpose(neigh_rows[:, at])
    weight_acc[...] = jnp.zeros_like(weight_acc)

    def turn(c):
        left_turned[0:cols, span(c)] = jnp.transpose(feat_full[f, span(c), :])

    loop(0, CHUNKS, turn)
    loop(0, parts - 1, take_blocks)

    def aggregate(c):
        agg_full[f, span(c), :] = (sum_ref[span(c), :] / deg_ref[span(c), 0:1]).astype(jnp.bfloat16)
        gather_start(1, agg_full, c)

    loop(0, CHUNKS, aggregate)
    loop(0, CHUNKS, lambda c: gather_relay(0, feat_full, c))

    def turn_aggregate(c):
        left_turned[cols:2 * cols, span(c)] = jnp.transpose(agg_full[f, span(c), :])


    def own_term(c):
        gather_finish(0, feat_full, c)
        total = dot(feat_full[0, span(c), :], self_cols[0:cols, :])
        for j in range(1, feats):
            total += dot(feat_full[j, span(c), :], self_cols[j * cols:(j + 1) * cols, :])
        pre_ref[span(c), :] = total

    loop(0, CHUNKS, own_term)
    loop(0, CHUNKS, turn_aggregate)

    def activate(c):
        gather_relay(1, agg_full, c)
        gather_finish(1, agg_full, c)
        total = pre_ref[span(c), :]
        for j in range(feats):
            total += dot(agg_full[j, span(c), :], neigh_cols[j * cols:(j + 1) * cols, :])
        sig = jax.nn.sigmoid(total)
        hidden_ref[span(c), :] = (total * sig).astype(jnp.bfloat16)
        slope = sig * (1.0 + total * (1.0 - sig))
        grad_full[f, span(c), :] = (cot_ref[span(c), :].astype(jnp.float32) * slope).astype(jnp.bfloat16)
        gather_start(2, grad_full, c)

    loop(0, CHUNKS, activate)
    hidden_copy = pltpu.make_async_copy(hidden_ref, hidden_hbm, o_sem.at[0])
    hidden_copy.start()

    def weight_grads(d, c):
        q = (x + d) % chips
        for k in range(2):
            at = slice(k * cols, (k + 1) * cols)
            weight_acc[d, :, at] += dot(left_turned[:, span(c)], grad_full[q * 2 + k, span(c), :])

    def back_rows(c):
        gather_relay(2, grad_full, c)
        gather_relayed(2, grad_full, c)
        total = dot(grad_full[0, span(c), :], neigh_turned[0:cols, :])
        for j in range(1, feats):
            total += dot(grad_full[j, span(c), :], neigh_turned[j * cols:(j + 1) * cols, :])
        back_ref[span(c), :] = (total / deg_ref[span(c), 0:1]).astype(jnp.bfloat16)

    tall = 2 * cols // parts

    def pieces():
        return [(a, b, (a * zs + b) * tall) for a in range(ys) for b in range(zs)]

    def y_copy(n, slot, to):
        return remote(y_out.at[n, to], y_in.at[n, slot], ys_send.at[n, to], ys_recv.at[n, slot], z * ys + to, f)

    def z_copy(n, slot, to):
        return remote(z_out.at[n, to], z_in.at[n, slot], zs_send.at[n, to], zs_recv.at[n, slot], to * ys + y, f)

    def z_gather(n, slot, to):
        piece = z_all.at[n, slot]
        return remote(piece, piece, za_send.at[n, to], za_recv.at[n, slot], to * ys + y, f)

    def y_gather(n, slot, to):
        piece = y_all.at[n, slot]
        return remote(piece, piece, ya_send.at[n, to], ya_recv.at[n, slot], z * ys + to, f)

    def reduce_start(n):
        for a, b, row in pieces():
            y_out[n, a, b] = weight_acc[n, row:row + tall, :].astype(jnp.bfloat16)
        for d in range(1, ys):
            y_copy(n, y, (y + d) % ys).start()
        y_in[n, y] = y_out[n, y]

    def reduce_z(n):
        for d in range(1, ys):
            p = (y + d) % ys
            y_copy(n, p, p).wait_recv()
        for b in range(zs):
            total = y_in[n, 0, b].astype(jnp.float32)
            for a in range(1, ys):
                total += y_in[n, a, b].astype(jnp.float32)
            z_out[n, b] = total.astype(jnp.bfloat16)
        for d in range(1, zs):
            z_copy(n, z, (z + d) % zs).start()
        z_in[n, z] = z_out[n, z]

    def finish_z(n):
        for d in range(1, zs):
            p = (z + d) % zs
            z_copy(n, p, p).wait_recv()
        total = z_in[n, 0].astype(jnp.float32)
        for b in range(1, zs):
            total += z_in[n, b].astype(jnp.float32)
        z_all[n, z] = total.astype(jnp.bfloat16)
        for d in range(1, zs):
            z_gather(n, z, (z + d) % zs).start()

    def finish_y(n):
        for d in range(1, zs):
            p = (z + d) % zs
            z_gather(n, p, p).wait_recv()
        y_all[n, y] = z_all[n]
        for d in range(1, ys):
            y_gather(n, y, (y + d) % ys).start()

    def write_grads(n):
        for d in range(1, ys):
            p = (y + d) % ys
            y_gather(n, p, p).wait_recv()
        at = pl.ds(pl.multiple_of((x + n) % chips * 2 * cols, 2 * cols), 2 * cols)
        for a, b, row in pieces():
            piece = y_all[n, a, b].astype(jnp.float32)
            if row < cols:
                grad_self_ref[row:row + tall, at] = piece
            else:
                grad_neigh_ref[row - cols:row - cols + tall, at] = piece

    def sibling_grads(c):
        arrival(2, grad_full, c, sibling).wait_recv()
        weight_grads(0, c)

    stages = (reduce_z, finish_z, finish_y)
    others = range(1, chips)
    loop(0, CHUNKS, sibling_grads)
    reduce_start(0)
    for c in range(CHUNKS):
        back_rows(c)
        for d in others:
            weight_grads(d, c)
        if c < len(stages):
            stages[c](0)

    def pick(p):
        ids = jnp.transpose(in_ids[p])[:, 0:1]
        total = jnp.zeros((cap, cols), jnp.float32)
        for c in range(CHUNKS):
            node = lax.broadcasted_iota(jnp.int32, (cap, chunk), 1) + c * chunk
            match = jnp.where(node == ids, 1.0, 0.0).astype(jnp.bfloat16)
            total += dot(match, back_ref[c * chunk:(c + 1) * chunk, :])
        return total.astype(jnp.bfloat16)

    def send_back(i):
        p = peer(i)
        back_out[p] = pick(p)
        return_copy(g, p).start()


    def keep(p):
        return pltpu.make_async_copy(back_in.at[p], returned_hbm.at[p], b_sem.at[p])

    for n in others:
        reduce_start(n)
    loop(0, half, send_back)
    for n in others:
        reduce_z(n)
    loop(half, parts - 1, send_back)
    back_in[g] = pick(g)
    keep(g).start()
    for n in others:
        finish_z(n)

    def self_part(c):
        total = dot(grad_full[0, span(c), :], self_turned[0:cols, :])
        for j in range(1, feats):
            total += dot(grad_full[j, span(c), :], self_turned[j * cols:(j + 1) * cols, :])
        self_grad_ref[span(c), :] = total

    loop(0, CHUNKS, self_part)
    self_copy = pltpu.make_async_copy(self_grad_ref, self_grad_hbm, o_sem.at[1])
    self_copy.start()
    write_grads(0)
    for n in others:
        finish_y(n)

    def returned(i):
        p = peer(parts - 2 - i)
        return_copy(p, p).wait_recv()
        keep(p).start()

    loop(0, parts - 1, returned)
    for n in others:
        write_grads(n)

    hidden_copy.wait()
    self_copy.wait()
    loop(0, parts, lambda p: keep(p).wait())

    def sent(d):
        p = (g + d) % parts
        id_copy(g, p).wait_send()
        block_copy(g, p).wait_send()
        return_copy(g, p).wait_send()

    loop(1, parts, sent)
    for n, full in enumerate((feat_full, agg_full, grad_full)):
        loop(0, CHUNKS, functools.partial(gather_sent, n, full))
    for n in range(chips):
        for d in range(1, ys):
            y_copy(n, y, (y + d) % ys).wait_send()
            y_gather(n, y, (y + d) % ys).wait_send()
        for d in range(1, zs):
            z_copy(n, z, (z + d) % zs).wait_send()
            z_gather(n, z, (z + d) % zs).wait_send()


def layer(send_counts, outgoing, send_rows, degrees, features, cotangent, w_self, w_neigh):
    parts, cap, cols = outgoing.shape
    nodes = features.shape[0]
    feats = lax.axis_size("feat")
    width = feats * cols
    ys = feats // 2
    zs = parts // ys
    chips = feats // 2
    tall, wide = 2 * cols // parts, 2 * cols
    bf16, f32 = jnp.bfloat16, jnp.float32
    dma = pltpu.SemaphoreType.DMA
    hops = max(feats // 2 - 1, 1)
    return pl.pallas_call(
        functools.partial(layer_kernel, parts, feats),
        out_shape=(
            jax.ShapeDtypeStruct((nodes, cols), bf16),
            jax.ShapeDtypeStruct((parts, cap, cols), bf16),
            jax.ShapeDtypeStruct((nodes, cols), f32),
            jax.ShapeDtypeStruct((cols, width), f32),
            jax.ShapeDtypeStruct((cols, width), f32),
        ),
        in_specs=[pl.BlockSpec(memory_space=SMEM)]
        + [pl.BlockSpec(memory_space=VMEM)] * 3
        + [pl.BlockSpec(memory_space=pl.ANY)] * 4,
        out_specs=[pl.BlockSpec(memory_space=pl.ANY)] * 3 + [pl.BlockSpec(memory_space=VMEM)] * 2,
        scratch_shapes=[
            pltpu.VMEM((parts, 8, cap), jnp.int32),
            pltpu.VMEM((nodes, 128), f32),
            pltpu.VMEM((nodes, cols), bf16),
            pltpu.VMEM((parts, cap, cols), bf16),
            pltpu.VMEM((parts, 8, cap), jnp.int32),
            pltpu.VMEM((nodes, cols), f32),
            pltpu.VMEM((nodes, cols), f32),
            pltpu.VMEM((feats, nodes, cols), bf16),
            pltpu.VMEM((feats, nodes, cols), bf16),
            pltpu.VMEM((feats, nodes, cols), bf16),
            pltpu.VMEM((nodes, cols), bf16),
            pltpu.VMEM((parts, cap, cols), bf16),
            pltpu.VMEM((parts, cap, cols), bf16),
            pltpu.VMEM((width, cols), bf16),
            pltpu.VMEM((width, cols), bf16),
            pltpu.VMEM((cols, width), bf16),
            pltpu.VMEM((cols, width), bf16),
            pltpu.VMEM((chips, 2 * cols, wide), f32),
            pltpu.VMEM((width, cols), bf16),
            pltpu.VMEM((width, cols), bf16),
            pltpu.VMEM((2 * cols, nodes), bf16),
            pltpu.VMEM((nodes, cols), bf16),
            pltpu.VMEM((nodes, cols), f32),
            pltpu.VMEM((chips, ys, zs, tall, wide), bf16),
            pltpu.VMEM((chips, ys, zs, tall, wide), bf16),
            pltpu.VMEM((chips, zs, tall, wide), bf16),
            pltpu.VMEM((chips, zs, tall, wide), bf16),
            pltpu.VMEM((chips, zs, tall, wide), bf16),
            pltpu.VMEM((chips, ys, zs, tall, wide), bf16),
            dma((parts,)), dma((parts,)), dma((parts,)), dma((parts,)), dma((parts,)), dma((parts,)),
            dma((5,)), dma((CHUNKS,)), dma((2,)), dma((parts,)),
            dma((3, hops, CHUNKS)), dma((3, CHUNKS)), dma((3, hops, CHUNKS)), dma((3, feats, CHUNKS)),
            dma((chips, ys)), dma((chips, ys)), dma((chips, zs)), dma((chips, zs)),
            dma((chips, zs)), dma((chips, zs)), dma((chips, ys)), dma((chips, ys)),
        ],
        compiler_params=pltpu.CompilerParams(
            collective_id=0, has_side_effects=True, vmem_limit_bytes=VMEM_BYTES
        ),
        name="layer",
    )(send_counts, outgoing, send_rows, degrees, features, cotangent, w_self, w_neigh)


def on_device(
    features,
    w_self,
    w_neigh,
    adjacency,
    block_source,
    block_to_slot,
    send_rows,
    send_counts,
    degree,
    cotangent,
):
    part_count = lax.axis_size("graph")
    feat_cols = features.shape[1]
    block_size = adjacency.shape[1]
    slot_cap = send_rows.shape[2]
    slot_total = part_count * slot_cap // block_size
    outgoing = collect(block_source, block_to_slot, send_counts, adjacency, features, slot_total)
    hidden, returned, self_grad, grad_self, grad_neigh = layer(
        send_counts, outgoing.reshape(part_count, slot_cap, feat_cols), send_rows,
        degree.reshape(-1, block_size), features, cotangent, w_self, w_neigh,
    )
    grad_features, hidden_out, grad_self, grad_neigh = spread(
        block_source, block_to_slot, adjacency,
        returned.reshape(slot_total, block_size, feat_cols), self_grad, hidden, grad_self, grad_neigh,
    )
    return (hidden_out, grad_features, grad_self, grad_neigh)


def solution(mesh):
    placed = (
        P("graph", "feat"),
        P(),
        P(),
        P("graph", None, None),
        P("graph"),
        P("graph"),
        P("graph", None, None),
        P("graph", None),
        P("graph"),
        P("graph", "feat"),
    )
    return jax.shard_map(
        on_device,
        mesh=mesh,
        in_specs=placed,
        out_specs=(P("graph", "feat"), P("graph", "feat"), P("feat", None), P("feat", None)),
        check_vma=False,
    )
```

```python
import functools

import jax
import jax.numpy as jnp
from jax import lax
from jax.experimental import pallas as pl
from jax.experimental.pallas import tpu as pltpu
from jax.sharding import PartitionSpec as P

SMEM = pltpu.SMEM
VMEM = pltpu.VMEM
MESH = pl.DeviceIdType.MESH
GROUP = 4
CHUNKS = 4
VMEM_BYTES = 60 * 2**20


def collect_kernel(source_ref, slot_ref, count_ref, adj_hbm, feat_hbm, out_ref, acc, adj_ref, feat_ref, sems):
    adj_copy = pltpu.make_async_copy(adj_hbm, adj_ref, sems.at[0])
    feat_copy = pltpu.make_async_copy(feat_hbm, feat_ref, sems.at[1])
    adj_copy.start()
    feat_copy.start()
    blocks, block, _ = adj_ref.shape
    slot_total = out_ref.shape[0]
    halves = slot_total // count_ref.shape[1]
    acc[...] = jnp.zeros_like(acc)
    adj_copy.wait()
    feat_copy.wait()

    def add(step, carry):
        prods = []
        for j in range(GROUP):
            k = step * GROUP + j
            rows = pl.ds(pl.multiple_of(source_ref[k] * block, block), block)
            prods.append(jnp.dot(adj_ref[k], feat_ref[rows, :], preferred_element_type=jnp.float32))
        for j in range(GROUP):
            acc[slot_ref[step * GROUP + j]] += prods[j]
        return carry

    lax.fori_loop(0, blocks // GROUP, add, 0)

    def finish(s, carry):
        limit = count_ref[0, s // halves] - (s % halves) * block
        rows = lax.broadcasted_iota(jnp.int32, out_ref.shape[1:], 0)
        out_ref[s] = jnp.where(rows < limit, acc[s], 0.0).astype(jnp.bfloat16)
        return carry

    lax.fori_loop(0, slot_total, finish, 0)


def collect(block_source, block_to_slot, send_counts, adjacency, features, slot_total):
    blocks, block, _ = adjacency.shape
    shape = (slot_total, block, features.shape[1])
    return pl.pallas_call(
        collect_kernel,
        out_shape=jax.ShapeDtypeStruct(shape, jnp.bfloat16),
        in_specs=[pl.BlockSpec(memory_space=SMEM)] * 3 + [pl.BlockSpec(memory_space=pl.ANY)] * 2,
        out_specs=pl.BlockSpec(memory_space=VMEM),
        scratch_shapes=[
            pltpu.VMEM(shape, jnp.float32),
            pltpu.VMEM(adjacency.shape, jnp.bfloat16),
            pltpu.VMEM(features.shape, jnp.bfloat16),
            pltpu.SemaphoreType.DMA((2,)),
        ],
        compiler_params=pltpu.CompilerParams(vmem_limit_bytes=VMEM_BYTES),
        name="collect",
    )(block_source, block_to_slot, send_counts, adjacency, features)


def spread_kernel(
    source_ref, slot_ref, adj_hbm, ret_hbm, start_hbm, hidden_in, self_in, neigh_in,
    out_ref, hidden_out, self_out, neigh_out, acc, adj_ref, ret_ref, hidden_ref, self_ref, neigh_ref, sems,
):
    loads = [
        pltpu.make_async_copy(adj_hbm, adj_ref, sems.at[0]),
        pltpu.make_async_copy(ret_hbm, ret_ref, sems.at[1]),
        pltpu.make_async_copy(start_hbm, acc, sems.at[2]),
    ]
    passed = [
        pltpu.make_async_copy(hidden_in, hidden_ref, sems.at[3]),
        pltpu.make_async_copy(self_in, self_ref, sems.at[4]),
        pltpu.make_async_copy(neigh_in, neigh_ref, sems.at[5]),
    ]
    results = [
        pltpu.make_async_copy(hidden_ref, hidden_out, sems.at[6]),
        pltpu.make_async_copy(self_ref, self_out, sems.at[7]),
        pltpu.make_async_copy(neigh_ref, neigh_out, sems.at[8]),
    ]
    for copy in loads + passed:
        copy.start()
    for copy in loads:
        copy.wait()
    for first, second in zip(passed, results):
        first.wait()
        second.start()
    blocks, block, _ = adj_ref.shape
    sources = out_ref.shape[0] // block

    def add(step, carry):
        prods = []
        for j in range(GROUP):
            k = step * GROUP + j
            prods.append(lax.dot_general(
                adj_ref[k], ret_ref[slot_ref[k]], (((0,), (0,)), ((), ())),
                preferred_element_type=jnp.float32,
            ))
        for j in range(GROUP):
            acc[source_ref[step * GROUP + j]] += prods[j]
        return carry

    lax.fori_loop(0, blocks // GROUP, add, 0)

    def finish(b, carry):
        rows = pl.ds(pl.multiple_of(b * block, block), block)
        out_ref[rows, :] = acc[b].astype(jnp.bfloat16)
        return carry

    lax.fori_loop(0, sources, finish, 0)
    for copy in results:
        copy.wait()


def spread(block_source, block_to_slot, adjacency, returned, self_grad, hidden, grad_self, grad_neigh):
    blocks, block, _ = adjacency.shape
    nodes, cols = self_grad.shape
    shape = (nodes // block, block, cols)
    passed = [jax.ShapeDtypeStruct(v.shape, v.dtype) for v in (hidden, grad_self, grad_neigh)]
    return pl.pallas_call(
        spread_kernel,
        out_shape=[jax.ShapeDtypeStruct((nodes, cols), jnp.bfloat16)] + passed,
        in_specs=[pl.BlockSpec(memory_space=SMEM)] * 2 + [pl.BlockSpec(memory_space=pl.ANY)] * 6,
        out_specs=[pl.BlockSpec(memory_space=VMEM)] + [pl.BlockSpec(memory_space=pl.ANY)] * 3,
        scratch_shapes=[
            pltpu.VMEM(shape, jnp.float32),
            pltpu.VMEM(adjacency.shape, jnp.bfloat16),
            pltpu.VMEM(returned.shape, jnp.bfloat16),
            pltpu.VMEM(hidden.shape, hidden.dtype),
            pltpu.VMEM(grad_self.shape, grad_self.dtype),
            pltpu.VMEM(grad_neigh.shape, grad_neigh.dtype),
            pltpu.SemaphoreType.DMA((9,)),
        ],
        compiler_params=pltpu.CompilerParams(vmem_limit_bytes=VMEM_BYTES),
        name="spread",
    )(block_source, block_to_slot, adjacency, returned, self_grad.reshape(shape), hidden, grad_self, grad_neigh)


def layer_kernel(
    parts, feats,
    count_ref, out_blocks, rows_ref, degree_ref, feat_hbm, cot_hbm, w_self, w_neigh,
    hidden_hbm, returned_hbm, self_grad_hbm, grad_self_ref, grad_neigh_ref,
    out_ids, deg_ref, cot_ref, in_blocks, in_ids, sum_ref, pre_ref, feat_full, agg_full, grad_full, back_ref, back_out, back_in,
    self_cols, neigh_cols, self_rows, neigh_rows, weight_acc,
    self_turned, neigh_turned, left_turned, hidden_ref, self_grad_ref,
    y_out, y_in, z_out, z_in, z_all, y_all,
    a_send, a_recv, i_send, i_recv, r_send, r_recv, w_sem, f_sem, o_sem, b_sem,
    gx_send, gs_send, gr_send, g_recv,
    ys_send, ys_recv, zs_send, zs_recv, za_send, za_recv, ya_send, ya_recv,
):
    g, f = lax.axis_index("graph"), lax.axis_index("feat")
    chips = feats // 2
    ys = chips
    zs = parts // ys
    x, core = f // 2, f % 2
    sibling = x * 2 + 1 - core
    z, y = g // ys, g % ys
    nodes, cols = feat_hbm.shape
    cap = out_blocks.shape[1]
    width = feats * cols
    chunk = nodes // CHUNKS

    def remote(src, dst, send, recv, graph_to, feat_to):
        return pltpu.make_async_remote_copy(
            src_ref=src, dst_ref=dst, send_sem=send, recv_sem=recv,
            device_id=(graph_to, feat_to), device_id_type=MESH,
        )

    def span(c):
        return pl.ds(pl.multiple_of(c * chunk, chunk), chunk)

    def loop(low, high, body):
        def step(i, carry):
            body(i)
            return carry

        lax.fori_loop(low, high, step, 0)

    def dot(a, b):
        return jnp.dot(a, b, preferred_element_type=jnp.float32)

    mine = pl.ds(pl.multiple_of(f * cols, cols), cols)
    weights = [
        pltpu.make_async_copy(w_self.at[:, mine], self_cols, w_sem.at[0]),
        pltpu.make_async_copy(w_neigh.at[:, mine], neigh_cols, w_sem.at[1]),
        pltpu.make_async_copy(w_self.at[mine, :], self_rows, w_sem.at[2]),
        pltpu.make_async_copy(w_neigh.at[mine, :], neigh_rows, w_sem.at[3]),
        pltpu.make_async_copy(cot_hbm, cot_ref, w_sem.at[4]),
    ]

    def feat_copy(c):
        return pltpu.make_async_copy(feat_hbm.at[span(c)], feat_full.at[f, span(c)], f_sem.at[c])

    loop(0, CHUNKS, lambda c: feat_copy(c).start())
    for w in weights:
        w.start()
    for p in range(parts):
        lane = lax.broadcasted_iota(jnp.int32, (8, cap), 1)
        ids = jnp.broadcast_to(rows_ref[0, p:p + 1, :], (8, cap))
        out_ids[p] = jnp.where(lane < count_ref[0, p], ids, -1)

    barrier = pltpu.get_barrier_semaphore()
    for d in range(1, parts):
        pl.semaphore_signal(barrier, inc=1, device_id=((g + d) % parts, f), device_id_type=MESH)
    for d in range(1, feats):
        pl.semaphore_signal(barrier, inc=1, device_id=(g, (f + d) % feats), device_id_type=MESH)
    pl.semaphore_wait(barrier, parts + feats - 2)

    def id_copy(slot, p):
        return remote(out_ids.at[p], in_ids.at[slot], i_send.at[p], i_recv.at[slot], p, f)

    def block_copy(slot, p):
        return remote(out_blocks.at[p], in_blocks.at[slot], a_send.at[p], a_recv.at[slot], p, f)

    def return_copy(slot, p):
        return remote(back_out.at[p], back_in.at[slot], r_send.at[p], r_recv.at[slot], p, f)

    half = parts // 2

    def peer(i):
        far = (1 - g // half) * half + (g + i) % half
        near = g // half * half + (g + i + 1 - half) % half
        return far * (1 - i // half) + near * (i // half)

    def send_blocks(i):
        p = peer(i)
        id_copy(g, p).start()
        block_copy(g, p).start()

    loop(0, parts - 1, send_blocks)

    def to_sibling(n, full, c):
        piece = full.at[f, span(c)]
        return remote(piece, piece, gs_send.at[n, c], g_recv.at[n, f, c], g, sibling)

    def to_chip(n, full, c, d):
        piece = full.at[f, span(c)]
        return remote(piece, piece, gx_send.at[n, d - 1, c], g_recv.at[n, f, c], g, (x + d) % chips * 2 + core)

    def relay(n, full, c, d):
        j = (x + d) % chips * 2 + core
        piece = full.at[j, span(c)]
        return remote(piece, piece, gr_send.at[n, d - 1, c], g_recv.at[n, j, c], g, sibling)

    def arrival(n, full, c, j):
        piece = full.at[j, span(c)]
        return remote(piece, piece, gs_send.at[n, c], g_recv.at[n, j, c], g, sibling)

    def gather_start(n, full, c):
        for d in range(1, chips):
            to_chip(n, full, c, d).start()
        to_sibling(n, full, c).start()

    def gather_relay(n, full, c):
        for d in range(1, chips):
            arrival(n, full, c, (x + d) % chips * 2 + core).wait_recv()
            relay(n, full, c, d).start()

    def gather_finish(n, full, c):
        arrival(n, full, c, sibling).wait_recv()
        gather_relayed(n, full, c)

    def gather_relayed(n, full, c):
        for d in range(1, chips):
            arrival(n, full, c, (x + d) % chips * 2 + 1 - core).wait_recv()

    def gather_sent(n, full, c):
        to_sibling(n, full, c).wait_send()
        for d in range(1, chips):
            to_chip(n, full, c, d).wait_send()
            relay(n, full, c, d).wait_send()

    def feat_start(c):
        feat_copy(c).wait()
        gather_start(0, feat_full, c)

    loop(0, CHUNKS, feat_start)
    columns = jnp.transpose(degree_ref[...].astype(jnp.float32))
    lanes = degree_ref.shape[1]
    for b in range(nodes // lanes):
        deg_ref[b * lanes:(b + 1) * lanes, :] = jnp.broadcast_to(columns[:, b:b + 1], (lanes, 128))

    def scatter(ids, values, first):
        def tile(c):
            node = lax.broadcasted_iota(jnp.int32, (chunk, cap), 0) + c * chunk
            match = jnp.where(node == ids, 1.0, 0.0).astype(jnp.bfloat16)
            added = dot(match, values)
            if first:
                sum_ref[span(c), :] = added
            else:
                sum_ref[span(c), :] += added

        loop(0, CHUNKS, tile)

    scatter(out_ids[g][0:1, :], out_blocks[g], True)
    in_ids[g] = out_ids[g]

    def take_blocks(i):
        p = peer(parts - 2 - i)
        id_copy(p, p).wait_recv()
        block_copy(p, p).wait_recv()
        scatter(in_ids[p][0:1, :], in_blocks[p], False)

    for w in weights:
        w.wait()
    for j in range(feats):
        at = slice(j * cols, (j + 1) * cols)
        self_turned[at, :] = jnp.transpose(self_rows[:, at])
        neigh_turned[at, :] = jnp.transpose(neigh_rows[:, at])
    weight_acc[...] = jnp.zeros_like(weight_acc)

    def turn(c):
        left_turned[0:cols, span(c)] = jnp.transpose(feat_full[f, span(c), :])

    loop(0, CHUNKS, turn)
    loop(0, parts - 1, take_blocks)

    def aggregate(c):
        agg_full[f, span(c), :] = (sum_ref[span(c), :] / deg_ref[span(c), 0:1]).astype(jnp.bfloat16)
        gather_start(1, agg_full, c)

    loop(0, CHUNKS, aggregate)
    loop(0, CHUNKS, lambda c: gather_relay(0, feat_full, c))

    def turn_aggregate(c):
        left_turned[cols:2 * cols, span(c)] = jnp.transpose(agg_full[f, span(c), :])


    def own_term(c):
        gather_finish(0, feat_full, c)
        total = dot(feat_full[0, span(c), :], self_cols[0:cols, :])
        for j in range(1, feats):
            total += dot(feat_full[j, span(c), :], self_cols[j * cols:(j + 1) * cols, :])
        pre_ref[span(c), :] = total

    loop(0, CHUNKS, own_term)
    loop(0, CHUNKS, turn_aggregate)

    def weight_grads(d, c):
        q = (x + d) % chips
        for k in range(2):
            at = slice(k * cols, (k + 1) * cols)
            weight_acc[d, :, at] += dot(left_turned[:, span(c)], grad_full[q * 2 + k, span(c), :])

    def sibling_grads(c):
        arrival(2, grad_full, c, sibling).wait_recv()
        weight_grads(0, c)

    def self_part(c):
        total = dot(grad_full[0, span(c), :], self_turned[0:cols, :])
        for j in range(1, feats):
            total += dot(grad_full[j, span(c), :], self_turned[j * cols:(j + 1) * cols, :])
        self_grad_ref[span(c), :] = total

    def activate(c):
        gather_relay(1, agg_full, c)
        gather_finish(1, agg_full, c)
        total = pre_ref[span(c), :]
        for j in range(feats):
            total += dot(agg_full[j, span(c), :], neigh_cols[j * cols:(j + 1) * cols, :])
        sig = jax.nn.sigmoid(total)
        hidden_ref[span(c), :] = (total * sig).astype(jnp.bfloat16)
        slope = sig * (1.0 + total * (1.0 - sig))
        grad_full[f, span(c), :] = (cot_ref[span(c), :].astype(jnp.float32) * slope).astype(jnp.bfloat16)
        gather_start(2, grad_full, c)

    activate(0)

    def activate_next(c):
        sibling_grads(c - 1)
        activate(c)

    loop(1, CHUNKS, activate_next)
    sibling_grads(CHUNKS - 1)
    hidden_copy = pltpu.make_async_copy(hidden_ref, hidden_hbm, o_sem.at[0])
    hidden_copy.start()

    def back_rows(c):
        gather_relay(2, grad_full, c)
        gather_relayed(2, grad_full, c)
        total = dot(grad_full[0, span(c), :], neigh_turned[0:cols, :])
        for j in range(1, feats):
            total += dot(grad_full[j, span(c), :], neigh_turned[j * cols:(j + 1) * cols, :])
        back_ref[span(c), :] = (total / deg_ref[span(c), 0:1]).astype(jnp.bfloat16)

    tall = 2 * cols // parts

    def pieces():
        return [(a, b, (a * zs + b) * tall) for a in range(ys) for b in range(zs)]

    def y_copy(n, slot, to):
        return remote(y_out.at[n, to], y_in.at[n, slot], ys_send.at[n, to], ys_recv.at[n, slot], z * ys + to, f)

    def z_copy(n, slot, to):
        return remote(z_out.at[n, to], z_in.at[n, slot], zs_send.at[n, to], zs_recv.at[n, slot], to * ys + y, f)

    def z_gather(n, slot, to):
        piece = z_all.at[n, slot]
        return remote(piece, piece, za_send.at[n, to], za_recv.at[n, slot], to * ys + y, f)

    def y_gather(n, slot, to):
        piece = y_all.at[n, slot]
        return remote(piece, piece, ya_send.at[n, to], ya_recv.at[n, slot], z * ys + to, f)

    def reduce_start(n):
        for a, b, row in pieces():
            y_out[n, a, b] = weight_acc[n, row:row + tall, :].astype(jnp.bfloat16)
        for d in range(1, ys):
            y_copy(n, y, (y + d) % ys).start()
        y_in[n, y] = y_out[n, y]

    def reduce_z(n):
        for d in range(1, ys):
            p = (y + d) % ys
            y_copy(n, p, p).wait_recv()
        for b in range(zs):
            total = y_in[n, 0, b].astype(jnp.float32)
            for a in range(1, ys):
                total += y_in[n, a, b].astype(jnp.float32)
            z_out[n, b] = total.astype(jnp.bfloat16)
        for d in range(1, zs):
            z_copy(n, z, (z + d) % zs).start()
        z_in[n, z] = z_out[n, z]

    def finish_z(n):
        for d in range(1, zs):
            p = (z + d) % zs
            z_copy(n, p, p).wait_recv()
        total = z_in[n, 0].astype(jnp.float32)
        for b in range(1, zs):
            total += z_in[n, b].astype(jnp.float32)
        z_all[n, z] = total.astype(jnp.bfloat16)
        for d in range(1, zs):
            z_gather(n, z, (z + d) % zs).start()

    def finish_y(n):
        for d in range(1, zs):
            p = (z + d) % zs
            z_gather(n, p, p).wait_recv()
        y_all[n, y] = z_all[n]
        for d in range(1, ys):
            y_gather(n, y, (y + d) % ys).start()

    def write_grads(n):
        for d in range(1, ys):
            p = (y + d) % ys
            y_gather(n, p, p).wait_recv()
        at = pl.ds(pl.multiple_of((x + n) % chips * 2 * cols, 2 * cols), 2 * cols)
        for a, b, row in pieces():
            piece = y_all[n, a, b].astype(jnp.float32)
            if row < cols:
                grad_self_ref[row:row + tall, at] = piece
            else:
                grad_neigh_ref[row - cols:row - cols + tall, at] = piece

    stages = (reduce_z, finish_z)
    others = range(1, chips)
    reduce_start(0)
    for c in range(CHUNKS):
        back_rows(c)
        for d in others:
            weight_grads(d, c)
        if c < len(stages):
            stages[c](0)
        if c < CHUNKS - 1:
            self_part(c)

    def pick(p):
        ids = jnp.transpose(in_ids[p])[:, 0:1]
        total = jnp.zeros((cap, cols), jnp.float32)
        for c in range(CHUNKS):
            node = lax.broadcasted_iota(jnp.int32, (cap, chunk), 1) + c * chunk
            match = jnp.where(node == ids, 1.0, 0.0).astype(jnp.bfloat16)
            total += dot(match, back_ref[c * chunk:(c + 1) * chunk, :])
        return total.astype(jnp.bfloat16)

    def send_back(i):
        p = peer(i)
        back_out[p] = pick(p)
        return_copy(g, p).start()


    def keep(p):
        return pltpu.make_async_copy(back_in.at[p], returned_hbm.at[p], b_sem.at[p])

    for n in others:
        reduce_start(n)
    loop(0, half, send_back)
    finish_y(0)
    for n in others:
        reduce_z(n)
    loop(half, parts - 1, send_back)
    back_in[g] = pick(g)
    keep(g).start()
    for n in others:
        finish_z(n)

    self_part(CHUNKS - 1)
    self_copy = pltpu.make_async_copy(self_grad_ref, self_grad_hbm, o_sem.at[1])
    self_copy.start()
    write_grads(0)
    for n in others:
        finish_y(n)

    def returned(i):
        p = peer(parts - 2 - i)
        return_copy(p, p).wait_recv()
        keep(p).start()

    loop(0, parts - 1, returned)
    for n in others:
        write_grads(n)

    hidden_copy.wait()
    self_copy.wait()
    loop(0, parts, lambda p: keep(p).wait())

    def sent(d):
        p = (g + d) % parts
        id_copy(g, p).wait_send()
        block_copy(g, p).wait_send()
        return_copy(g, p).wait_send()

    loop(1, parts, sent)
    for n, full in enumerate((feat_full, agg_full, grad_full)):
        loop(0, CHUNKS, functools.partial(gather_sent, n, full))
    for n in range(chips):
        for d in range(1, ys):
            y_copy(n, y, (y + d) % ys).wait_send()
            y_gather(n, y, (y + d) % ys).wait_send()
        for d in range(1, zs):
            z_copy(n, z, (z + d) % zs).wait_send()
            z_gather(n, z, (z + d) % zs).wait_send()


def layer(send_counts, outgoing, send_rows, degrees, features, cotangent, w_self, w_neigh):
    parts, cap, cols = outgoing.shape
    nodes = features.shape[0]
    feats = lax.axis_size("feat")
    width = feats * cols
    ys = feats // 2
    zs = parts // ys
    chips = feats // 2
    tall, wide = 2 * cols // parts, 2 * cols
    bf16, f32 = jnp.bfloat16, jnp.float32
    dma = pltpu.SemaphoreType.DMA
    hops = max(feats // 2 - 1, 1)
    return pl.pallas_call(
        functools.partial(layer_kernel, parts, feats),
        out_shape=(
            jax.ShapeDtypeStruct((nodes, cols), bf16),
            jax.ShapeDtypeStruct((parts, cap, cols), bf16),
            jax.ShapeDtypeStruct((nodes, cols), f32),
            jax.ShapeDtypeStruct((cols, width), f32),
            jax.ShapeDtypeStruct((cols, width), f32),
        ),
        in_specs=[pl.BlockSpec(memory_space=SMEM)]
        + [pl.BlockSpec(memory_space=VMEM)] * 3
        + [pl.BlockSpec(memory_space=pl.ANY)] * 4,
        out_specs=[pl.BlockSpec(memory_space=pl.ANY)] * 3 + [pl.BlockSpec(memory_space=VMEM)] * 2,
        scratch_shapes=[
            pltpu.VMEM((parts, 8, cap), jnp.int32),
            pltpu.VMEM((nodes, 128), f32),
            pltpu.VMEM((nodes, cols), bf16),
            pltpu.VMEM((parts, cap, cols), bf16),
            pltpu.VMEM((parts, 8, cap), jnp.int32),
            pltpu.VMEM((nodes, cols), f32),
            pltpu.VMEM((nodes, cols), f32),
            pltpu.VMEM((feats, nodes, cols), bf16),
            pltpu.VMEM((feats, nodes, cols), bf16),
            pltpu.VMEM((feats, nodes, cols), bf16),
            pltpu.VMEM((nodes, cols), bf16),
            pltpu.VMEM((parts, cap, cols), bf16),
            pltpu.VMEM((parts, cap, cols), bf16),
            pltpu.VMEM((width, cols), bf16),
            pltpu.VMEM((width, cols), bf16),
            pltpu.VMEM((cols, width), bf16),
            pltpu.VMEM((cols, width), bf16),
            pltpu.VMEM((chips, 2 * cols, wide), f32),
            pltpu.VMEM((width, cols), bf16),
            pltpu.VMEM((width, cols), bf16),
            pltpu.VMEM((2 * cols, nodes), bf16),
            pltpu.VMEM((nodes, cols), bf16),
            pltpu.VMEM((nodes, cols), f32),
            pltpu.VMEM((chips, ys, zs, tall, wide), bf16),
            pltpu.VMEM((chips, ys, zs, tall, wide), bf16),
            pltpu.VMEM((chips, zs, tall, wide), bf16),
            pltpu.VMEM((chips, zs, tall, wide), bf16),
            pltpu.VMEM((chips, zs, tall, wide), bf16),
            pltpu.VMEM((chips, ys, zs, tall, wide), bf16),
            dma((parts,)), dma((parts,)), dma((parts,)), dma((parts,)), dma((parts,)), dma((parts,)),
            dma((5,)), dma((CHUNKS,)), dma((2,)), dma((parts,)),
            dma((3, hops, CHUNKS)), dma((3, CHUNKS)), dma((3, hops, CHUNKS)), dma((3, feats, CHUNKS)),
            dma((chips, ys)), dma((chips, ys)), dma((chips, zs)), dma((chips, zs)),
            dma((chips, zs)), dma((chips, zs)), dma((chips, ys)), dma((chips, ys)),
        ],
        compiler_params=pltpu.CompilerParams(
            collective_id=0, has_side_effects=True, vmem_limit_bytes=VMEM_BYTES
        ),
        name="layer",
    )(send_counts, outgoing, send_rows, degrees, features, cotangent, w_self, w_neigh)


def on_device(
    features,
    w_self,
    w_neigh,
    adjacency,
    block_source,
    block_to_slot,
    send_rows,
    send_counts,
    degree,
    cotangent,
):
    part_count = lax.axis_size("graph")
    feat_cols = features.shape[1]
    block_size = adjacency.shape[1]
    slot_cap = send_rows.shape[2]
    slot_total = part_count * slot_cap // block_size
    outgoing = collect(block_source, block_to_slot, send_counts, adjacency, features, slot_total)
    hidden, returned, self_grad, grad_self, grad_neigh = layer(
        send_counts, outgoing.reshape(part_count, slot_cap, feat_cols), send_rows,
        degree.reshape(-1, block_size), features, cotangent, w_self, w_neigh,
    )
    grad_features, hidden_out, grad_self, grad_neigh = spread(
        block_source, block_to_slot, adjacency,
        returned.reshape(slot_total, block_size, feat_cols), self_grad, hidden, grad_self, grad_neigh,
    )
    return (hidden_out, grad_features, grad_self, grad_neigh)


def solution(mesh):
    placed = (
        P("graph", "feat"),
        P(),
        P(),
        P("graph", None, None),
        P("graph"),
        P("graph"),
        P("graph", None, None),
        P("graph", None),
        P("graph"),
        P("graph", "feat"),
    )
    return jax.shard_map(
        on_device,
        mesh=mesh,
        in_specs=placed,
        out_specs=(P("graph", "feat"), P("graph", "feat"), P("feat", None), P("feat", None)),
        check_vma=False,
    )
```

```python
import functools

import jax
import jax.numpy as jnp
from jax import lax
from jax.experimental import pallas as pl
from jax.experimental.pallas import tpu as pltpu
from jax.sharding import PartitionSpec as P

SMEM = pltpu.SMEM
VMEM = pltpu.VMEM
MESH = pl.DeviceIdType.MESH
GROUP = 4
CHUNKS = 4
VMEM_BYTES = 60 * 2**20


def collect_kernel(source_ref, slot_ref, count_ref, adj_hbm, feat_hbm, out_ref, acc, adj_ref, feat_ref, sems):
    adj_copy = pltpu.make_async_copy(adj_hbm, adj_ref, sems.at[0])
    feat_copy = pltpu.make_async_copy(feat_hbm, feat_ref, sems.at[1])
    adj_copy.start()
    feat_copy.start()
    blocks, block, _ = adj_ref.shape
    slot_total = out_ref.shape[0]
    halves = slot_total // count_ref.shape[1]
    acc[...] = jnp.zeros_like(acc)
    adj_copy.wait()
    feat_copy.wait()

    def add(step, carry):
        prods = []
        for j in range(GROUP):
            k = step * GROUP + j
            rows = pl.ds(pl.multiple_of(source_ref[k] * block, block), block)
            prods.append(jnp.dot(adj_ref[k], feat_ref[rows, :], preferred_element_type=jnp.float32))
        for j in range(GROUP):
            acc[slot_ref[step * GROUP + j]] += prods[j]
        return carry

    lax.fori_loop(0, blocks // GROUP, add, 0)

    def finish(s, carry):
        limit = count_ref[0, s // halves] - (s % halves) * block
        rows = lax.broadcasted_iota(jnp.int32, out_ref.shape[1:], 0)
        out_ref[s] = jnp.where(rows < limit, acc[s], 0.0).astype(jnp.bfloat16)
        return carry

    lax.fori_loop(0, slot_total, finish, 0)


def collect(block_source, block_to_slot, send_counts, adjacency, features, slot_total):
    blocks, block, _ = adjacency.shape
    shape = (slot_total, block, features.shape[1])
    return pl.pallas_call(
        collect_kernel,
        out_shape=jax.ShapeDtypeStruct(shape, jnp.bfloat16),
        in_specs=[pl.BlockSpec(memory_space=SMEM)] * 3 + [pl.BlockSpec(memory_space=pl.ANY)] * 2,
        out_specs=pl.BlockSpec(memory_space=VMEM),
        scratch_shapes=[
            pltpu.VMEM(shape, jnp.float32),
            pltpu.VMEM(adjacency.shape, jnp.bfloat16),
            pltpu.VMEM(features.shape, jnp.bfloat16),
            pltpu.SemaphoreType.DMA((2,)),
        ],
        compiler_params=pltpu.CompilerParams(vmem_limit_bytes=VMEM_BYTES),
        name="collect",
    )(block_source, block_to_slot, send_counts, adjacency, features)


def spread_kernel(
    source_ref, slot_ref, adj_hbm, ret_hbm, start_hbm, hidden_in, self_in, neigh_in,
    out_ref, hidden_out, self_out, neigh_out, acc, adj_ref, ret_ref, hidden_ref, self_ref, neigh_ref, sems,
):
    loads = [
        pltpu.make_async_copy(adj_hbm, adj_ref, sems.at[0]),
        pltpu.make_async_copy(ret_hbm, ret_ref, sems.at[1]),
        pltpu.make_async_copy(start_hbm, acc, sems.at[2]),
    ]
    passed = [
        pltpu.make_async_copy(hidden_in, hidden_ref, sems.at[3]),
        pltpu.make_async_copy(self_in, self_ref, sems.at[4]),
        pltpu.make_async_copy(neigh_in, neigh_ref, sems.at[5]),
    ]
    results = [
        pltpu.make_async_copy(hidden_ref, hidden_out, sems.at[6]),
        pltpu.make_async_copy(self_ref, self_out, sems.at[7]),
        pltpu.make_async_copy(neigh_ref, neigh_out, sems.at[8]),
    ]
    for copy in loads:
        copy.start()
    for copy in loads:
        copy.wait()
    for copy in passed:
        copy.start()
    for first, second in zip(passed, results):
        first.wait()
        second.start()
    blocks, block, _ = adj_ref.shape
    sources = out_ref.shape[0] // block

    def add(step, carry):
        prods = []
        for j in range(GROUP):
            k = step * GROUP + j
            prods.append(lax.dot_general(
                adj_ref[k], ret_ref[slot_ref[k]], (((0,), (0,)), ((), ())),
                preferred_element_type=jnp.float32,
            ))
        for j in range(GROUP):
            acc[source_ref[step * GROUP + j]] += prods[j]
        return carry

    lax.fori_loop(0, blocks // GROUP, add, 0)

    def finish(b, carry):
        rows = pl.ds(pl.multiple_of(b * block, block), block)
        out_ref[rows, :] = acc[b].astype(jnp.bfloat16)
        return carry

    lax.fori_loop(0, sources, finish, 0)
    for copy in results:
        copy.wait()


def spread(block_source, block_to_slot, adjacency, returned, self_grad, hidden, grad_self, grad_neigh):
    blocks, block, _ = adjacency.shape
    nodes, cols = self_grad.shape
    shape = (nodes // block, block, cols)
    passed = [jax.ShapeDtypeStruct(v.shape, v.dtype) for v in (hidden, grad_self, grad_neigh)]
    return pl.pallas_call(
        spread_kernel,
        out_shape=[jax.ShapeDtypeStruct((nodes, cols), jnp.bfloat16)] + passed,
        in_specs=[pl.BlockSpec(memory_space=SMEM)] * 2 + [pl.BlockSpec(memory_space=pl.ANY)] * 6,
        out_specs=[pl.BlockSpec(memory_space=VMEM)] + [pl.BlockSpec(memory_space=pl.ANY)] * 3,
        scratch_shapes=[
            pltpu.VMEM(shape, jnp.float32),
            pltpu.VMEM(adjacency.shape, jnp.bfloat16),
            pltpu.VMEM(returned.shape, jnp.bfloat16),
            pltpu.VMEM(hidden.shape, hidden.dtype),
            pltpu.VMEM(grad_self.shape, grad_self.dtype),
            pltpu.VMEM(grad_neigh.shape, grad_neigh.dtype),
            pltpu.SemaphoreType.DMA((9,)),
        ],
        compiler_params=pltpu.CompilerParams(vmem_limit_bytes=VMEM_BYTES),
        name="spread",
    )(block_source, block_to_slot, adjacency, returned, self_grad.reshape(shape), hidden, grad_self, grad_neigh)


def layer_kernel(
    parts, feats,
    count_ref, out_blocks, rows_ref, degree_ref, feat_hbm, cot_hbm, w_self, w_neigh,
    hidden_hbm, returned_hbm, self_grad_hbm, grad_self_ref, grad_neigh_ref,
    out_ids, deg_ref, cot_ref, in_blocks, in_ids, sum_ref, pre_ref, feat_full, agg_full, grad_full, back_ref, back_out, back_in,
    self_cols, neigh_cols, self_rows, neigh_rows, weight_acc,
    self_turned, neigh_turned, left_turned, hidden_ref, self_grad_ref,
    y_out, y_in, z_out, z_in, z_all, y_all,
    a_send, a_recv, i_send, i_recv, r_send, r_recv, w_sem, f_sem, o_sem, b_sem,
    gx_send, gs_send, gr_send, g_recv,
    ys_send, ys_recv, zs_send, zs_recv, za_send, za_recv, ya_send, ya_recv,
):
    g, f = lax.axis_index("graph"), lax.axis_index("feat")
    chips = feats // 2
    ys = chips
    zs = parts // ys
    x, core = f // 2, f % 2
    sibling = x * 2 + 1 - core
    z, y = g // ys, g % ys
    nodes, cols = feat_hbm.shape
    cap = out_blocks.shape[1]
    width = feats * cols
    chunk = nodes // CHUNKS

    def remote(src, dst, send, recv, graph_to, feat_to):
        return pltpu.make_async_remote_copy(
            src_ref=src, dst_ref=dst, send_sem=send, recv_sem=recv,
            device_id=(graph_to, feat_to), device_id_type=MESH,
        )

    def span(c):
        return pl.ds(pl.multiple_of(c * chunk, chunk), chunk)

    def loop(low, high, body):
        def step(i, carry):
            body(i)
            return carry

        lax.fori_loop(low, high, step, 0)

    def dot(a, b):
        return jnp.dot(a, b, preferred_element_type=jnp.float32)

    mine = pl.ds(pl.multiple_of(f * cols, cols), cols)
    weights = [
        pltpu.make_async_copy(w_self.at[:, mine], self_cols, w_sem.at[0]),
        pltpu.make_async_copy(w_neigh.at[:, mine], neigh_cols, w_sem.at[1]),
        pltpu.make_async_copy(w_self.at[mine, :], self_rows, w_sem.at[2]),
        pltpu.make_async_copy(w_neigh.at[mine, :], neigh_rows, w_sem.at[3]),
        pltpu.make_async_copy(cot_hbm, cot_ref, w_sem.at[4]),
    ]

    def feat_copy(c):
        return pltpu.make_async_copy(feat_hbm.at[span(c)], feat_full.at[f, span(c)], f_sem.at[c])

    loop(0, CHUNKS, lambda c: feat_copy(c).start())
    for w in weights:
        w.start()
    for p in range(parts):
        lane = lax.broadcasted_iota(jnp.int32, (8, cap), 1)
        ids = jnp.broadcast_to(rows_ref[0, p:p + 1, :], (8, cap))
        out_ids[p] = jnp.where(lane < count_ref[0, p], ids, -1)

    barrier = pltpu.get_barrier_semaphore()
    for d in range(1, parts):
        pl.semaphore_signal(barrier, inc=1, device_id=((g + d) % parts, f), device_id_type=MESH)
    for d in range(1, feats):
        pl.semaphore_signal(barrier, inc=1, device_id=(g, (f + d) % feats), device_id_type=MESH)
    pl.semaphore_wait(barrier, parts + feats - 2)

    def id_copy(slot, p):
        return remote(out_ids.at[p], in_ids.at[slot], i_send.at[p], i_recv.at[slot], p, f)

    def block_copy(slot, p):
        return remote(out_blocks.at[p], in_blocks.at[slot], a_send.at[p], a_recv.at[slot], p, f)

    def return_copy(slot, p):
        return remote(back_out.at[p], back_in.at[slot], r_send.at[p], r_recv.at[slot], p, f)

    half = parts // 2

    def peer(i):
        far = (1 - g // half) * half + (g + i) % half
        near = g // half * half + (g + i + 1 - half) % half
        return far * (1 - i // half) + near * (i // half)

    def send_blocks(i):
        p = peer(i)
        id_copy(g, p).start()
        block_copy(g, p).start()

    loop(0, parts - 1, send_blocks)

    def to_sibling(n, full, c):
        piece = full.at[f, span(c)]
        return remote(piece, piece, gs_send.at[n, c], g_recv.at[n, f, c], g, sibling)

    def to_chip(n, full, c, d):
        piece = full.at[f, span(c)]
        return remote(piece, piece, gx_send.at[n, d - 1, c], g_recv.at[n, f, c], g, (x + d) % chips * 2 + core)

    def relay(n, full, c, d):
        j = (x + d) % chips * 2 + core
        piece = full.at[j, span(c)]
        return remote(piece, piece, gr_send.at[n, d - 1, c], g_recv.at[n, j, c], g, sibling)

    def arrival(n, full, c, j):
        piece = full.at[j, span(c)]
        return remote(piece, piece, gs_send.at[n, c], g_recv.at[n, j, c], g, sibling)

    def gather_start(n, full, c):
        for d in range(1, chips):
            to_chip(n, full, c, d).start()
        to_sibling(n, full, c).start()

    def gather_relay(n, full, c):
        for d in range(1, chips):
            arrival(n, full, c, (x + d) % chips * 2 + core).wait_recv()
            relay(n, full, c, d).start()

    def gather_finish(n, full, c):
        arrival(n, full, c, sibling).wait_recv()
        gather_relayed(n, full, c)

    def gather_relayed(n, full, c):
        for d in range(1, chips):
            arrival(n, full, c, (x + d) % chips * 2 + 1 - core).wait_recv()

    def gather_sent(n, full, c):
        to_sibling(n, full, c).wait_send()
        for d in range(1, chips):
            to_chip(n, full, c, d).wait_send()
            relay(n, full, c, d).wait_send()

    def feat_start(c):
        feat_copy(c).wait()
        gather_start(0, feat_full, c)

    loop(0, CHUNKS, feat_start)
    columns = jnp.transpose(degree_ref[...].astype(jnp.float32))
    lanes = degree_ref.shape[1]
    for b in range(nodes // lanes):
        deg_ref[b * lanes:(b + 1) * lanes, :] = jnp.broadcast_to(columns[:, b:b + 1], (lanes, 128))

    def scatter(ids, values, first):
        def tile(c):
            node = lax.broadcasted_iota(jnp.int32, (chunk, cap), 0) + c * chunk
            match = jnp.where(node == ids, 1.0, 0.0).astype(jnp.bfloat16)
            added = dot(match, values)
            if first:
                sum_ref[span(c), :] = added
            else:
                sum_ref[span(c), :] += added

        loop(0, CHUNKS, tile)

    scatter(out_ids[g][0:1, :], out_blocks[g], True)
    in_ids[g] = out_ids[g]

    def take_blocks(i):
        p = peer(parts - 2 - i)
        id_copy(p, p).wait_recv()
        block_copy(p, p).wait_recv()
        scatter(in_ids[p][0:1, :], in_blocks[p], False)

    for w in weights:
        w.wait()
    for j in range(feats):
        at = slice(j * cols, (j + 1) * cols)
        self_turned[at, :] = jnp.transpose(self_rows[:, at])
        neigh_turned[at, :] = jnp.transpose(neigh_rows[:, at])
    weight_acc[...] = jnp.zeros_like(weight_acc)

    def turn(c):
        left_turned[0:cols, span(c)] = jnp.transpose(feat_full[f, span(c), :])

    loop(0, CHUNKS, turn)
    loop(0, parts - 1, take_blocks)

    def aggregate(c):
        agg_full[f, span(c), :] = (sum_ref[span(c), :] / deg_ref[span(c), 0:1]).astype(jnp.bfloat16)
        gather_start(1, agg_full, c)

    loop(0, CHUNKS, aggregate)
    loop(0, CHUNKS, lambda c: gather_relay(0, feat_full, c))

    def turn_aggregate(c):
        left_turned[cols:2 * cols, span(c)] = jnp.transpose(agg_full[f, span(c), :])


    def own_term(c):
        gather_finish(0, feat_full, c)
        total = dot(feat_full[0, span(c), :], self_cols[0:cols, :])
        for j in range(1, feats):
            total += dot(feat_full[j, span(c), :], self_cols[j * cols:(j + 1) * cols, :])
        pre_ref[span(c), :] = total

    loop(0, CHUNKS, own_term)
    loop(0, CHUNKS, turn_aggregate)

    def weight_grads(d, c):
        q = (x + d) % chips
        for k in range(2):
            at = slice(k * cols, (k + 1) * cols)
            weight_acc[d, :, at] += dot(left_turned[:, span(c)], grad_full[q * 2 + k, span(c), :])

    def sibling_grads(c):
        arrival(2, grad_full, c, sibling).wait_recv()
        weight_grads(0, c)

    def self_part(c):
        total = dot(grad_full[0, span(c), :], self_turned[0:cols, :])
        for j in range(1, feats):
            total += dot(grad_full[j, span(c), :], self_turned[j * cols:(j + 1) * cols, :])
        self_grad_ref[span(c), :] = total

    def activate(c):
        gather_relay(1, agg_full, c)
        gather_finish(1, agg_full, c)
        total = pre_ref[span(c), :]
        for j in range(feats):
            total += dot(agg_full[j, span(c), :], neigh_cols[j * cols:(j + 1) * cols, :])
        sig = jax.nn.sigmoid(total)
        hidden_ref[span(c), :] = (total * sig).astype(jnp.bfloat16)
        slope = sig * (1.0 + total * (1.0 - sig))
        grad_full[f, span(c), :] = (cot_ref[span(c), :].astype(jnp.float32) * slope).astype(jnp.bfloat16)
        gather_start(2, grad_full, c)

    activate(0)

    def activate_next(c):
        sibling_grads(c - 1)
        activate(c)

    loop(1, CHUNKS, activate_next)
    sibling_grads(CHUNKS - 1)
    hidden_copy = pltpu.make_async_copy(hidden_ref, hidden_hbm, o_sem.at[0])
    hidden_copy.start()

    def back_rows(c):
        gather_relay(2, grad_full, c)
        gather_relayed(2, grad_full, c)
        total = dot(grad_full[0, span(c), :], neigh_turned[0:cols, :])
        for j in range(1, feats):
            total += dot(grad_full[j, span(c), :], neigh_turned[j * cols:(j + 1) * cols, :])
        back_ref[span(c), :] = (total / deg_ref[span(c), 0:1]).astype(jnp.bfloat16)

    tall = 2 * cols // parts

    def pieces():
        return [(a, b, (a * zs + b) * tall) for a in range(ys) for b in range(zs)]

    def y_copy(n, slot, to):
        return remote(y_out.at[n, to], y_in.at[n, slot], ys_send.at[n, to], ys_recv.at[n, slot], z * ys + to, f)

    def z_copy(n, slot, to):
        return remote(z_out.at[n, to], z_in.at[n, slot], zs_send.at[n, to], zs_recv.at[n, slot], to * ys + y, f)

    def z_gather(n, slot, to):
        piece = z_all.at[n, slot]
        return remote(piece, piece, za_send.at[n, to], za_recv.at[n, slot], to * ys + y, f)

    def y_gather(n, slot, to):
        piece = y_all.at[n, slot]
        return remote(piece, piece, ya_send.at[n, to], ya_recv.at[n, slot], z * ys + to, f)

    def reduce_start(n):
        for a, b, row in pieces():
            y_out[n, a, b] = weight_acc[n, row:row + tall, :].astype(jnp.bfloat16)
        for d in range(1, ys):
            y_copy(n, y, (y + d) % ys).start()
        y_in[n, y] = y_out[n, y]

    def reduce_z(n):
        for d in range(1, ys):
            p = (y + d) % ys
            y_copy(n, p, p).wait_recv()
        for b in range(zs):
            total = y_in[n, 0, b].astype(jnp.float32)
            for a in range(1, ys):
                total += y_in[n, a, b].astype(jnp.float32)
            z_out[n, b] = total.astype(jnp.bfloat16)
        for d in range(1, zs):
            z_copy(n, z, (z + d) % zs).start()
        z_in[n, z] = z_out[n, z]

    def finish_z(n):
        for d in range(1, zs):
            p = (z + d) % zs
            z_copy(n, p, p).wait_recv()
        total = z_in[n, 0].astype(jnp.float32)
        for b in range(1, zs):
            total += z_in[n, b].astype(jnp.float32)
        z_all[n, z] = total.astype(jnp.bfloat16)
        for d in range(1, zs):
            z_gather(n, z, (z + d) % zs).start()

    def finish_y(n):
        for d in range(1, zs):
            p = (z + d) % zs
            z_gather(n, p, p).wait_recv()
        y_all[n, y] = z_all[n]
        for d in range(1, ys):
            y_gather(n, y, (y + d) % ys).start()

    def write_grads(n):
        for d in range(1, ys):
            p = (y + d) % ys
            y_gather(n, p, p).wait_recv()
        at = pl.ds(pl.multiple_of((x + n) % chips * 2 * cols, 2 * cols), 2 * cols)
        for a, b, row in pieces():
            piece = y_all[n, a, b].astype(jnp.float32)
            if row < cols:
                grad_self_ref[row:row + tall, at] = piece
            else:
                grad_neigh_ref[row - cols:row - cols + tall, at] = piece

    stages = (reduce_z, finish_z)
    others = range(1, chips)
    reduce_start(0)
    for c in range(CHUNKS):
        back_rows(c)
        for d in others:
            weight_grads(d, c)
        if c < len(stages):
            stages[c](0)
        if c < CHUNKS - 1:
            self_part(c)

    def pick(p):
        ids = jnp.transpose(in_ids[p])[:, 0:1]
        total = jnp.zeros((cap, cols), jnp.float32)
        for c in range(CHUNKS):
            node = lax.broadcasted_iota(jnp.int32, (cap, chunk), 1) + c * chunk
            match = jnp.where(node == ids, 1.0, 0.0).astype(jnp.bfloat16)
            total += dot(match, back_ref[c * chunk:(c + 1) * chunk, :])
        return total.astype(jnp.bfloat16)

    def send_back(i):
        p = peer(i)
        back_out[p] = pick(p)
        return_copy(g, p).start()


    def keep(p):
        return pltpu.make_async_copy(back_in.at[p], returned_hbm.at[p], b_sem.at[p])

    for n in others:
        reduce_start(n)
    loop(0, half - 1, send_back)
    finish_y(0)
    for n in others:
        reduce_z(n)
    loop(half, parts - 1, send_back)
    back_in[g] = pick(g)
    keep(g).start()
    for n in others:
        finish_z(n)
    send_back(half - 1)

    self_part(CHUNKS - 1)
    self_copy = pltpu.make_async_copy(self_grad_ref, self_grad_hbm, o_sem.at[1])
    self_copy.start()
    write_grads(0)
    for n in others:
        finish_y(n)

    def returned(i):
        p = peer(parts - 2 - i)
        return_copy(p, p).wait_recv()
        keep(p).start()

    loop(0, parts - 1, returned)
    for n in others:
        write_grads(n)

    hidden_copy.wait()
    self_copy.wait()
    loop(0, parts, lambda p: keep(p).wait())

    def sent(d):
        p = (g + d) % parts
        id_copy(g, p).wait_send()
        block_copy(g, p).wait_send()
        return_copy(g, p).wait_send()

    loop(1, parts, sent)
    for n, full in enumerate((feat_full, agg_full, grad_full)):
        loop(0, CHUNKS, functools.partial(gather_sent, n, full))
    for n in range(chips):
        for d in range(1, ys):
            y_copy(n, y, (y + d) % ys).wait_send()
            y_gather(n, y, (y + d) % ys).wait_send()
        for d in range(1, zs):
            z_copy(n, z, (z + d) % zs).wait_send()
            z_gather(n, z, (z + d) % zs).wait_send()


def layer(send_counts, outgoing, send_rows, degrees, features, cotangent, w_self, w_neigh):
    parts, cap, cols = outgoing.shape
    nodes = features.shape[0]
    feats = lax.axis_size("feat")
    width = feats * cols
    ys = feats // 2
    zs = parts // ys
    chips = feats // 2
    tall, wide = 2 * cols // parts, 2 * cols
    bf16, f32 = jnp.bfloat16, jnp.float32
    dma = pltpu.SemaphoreType.DMA
    hops = max(feats // 2 - 1, 1)
    return pl.pallas_call(
        functools.partial(layer_kernel, parts, feats),
        out_shape=(
            jax.ShapeDtypeStruct((nodes, cols), bf16),
            jax.ShapeDtypeStruct((parts, cap, cols), bf16),
            jax.ShapeDtypeStruct((nodes, cols), f32),
            jax.ShapeDtypeStruct((cols, width), f32),
            jax.ShapeDtypeStruct((cols, width), f32),
        ),
        in_specs=[pl.BlockSpec(memory_space=SMEM)]
        + [pl.BlockSpec(memory_space=VMEM)] * 3
        + [pl.BlockSpec(memory_space=pl.ANY)] * 4,
        out_specs=[pl.BlockSpec(memory_space=pl.ANY)] * 3 + [pl.BlockSpec(memory_space=VMEM)] * 2,
        scratch_shapes=[
            pltpu.VMEM((parts, 8, cap), jnp.int32),
            pltpu.VMEM((nodes, 128), f32),
            pltpu.VMEM((nodes, cols), bf16),
            pltpu.VMEM((parts, cap, cols), bf16),
            pltpu.VMEM((parts, 8, cap), jnp.int32),
            pltpu.VMEM((nodes, cols), f32),
            pltpu.VMEM((nodes, cols), f32),
            pltpu.VMEM((feats, nodes, cols), bf16),
            pltpu.VMEM((feats, nodes, cols), bf16),
            pltpu.VMEM((feats, nodes, cols), bf16),
            pltpu.VMEM((nodes, cols), bf16),
            pltpu.VMEM((parts, cap, cols), bf16),
            pltpu.VMEM((parts, cap, cols), bf16),
            pltpu.VMEM((width, cols), bf16),
            pltpu.VMEM((width, cols), bf16),
            pltpu.VMEM((cols, width), bf16),
            pltpu.VMEM((cols, width), bf16),
            pltpu.VMEM((chips, 2 * cols, wide), f32),
            pltpu.VMEM((width, cols), bf16),
            pltpu.VMEM((width, cols), bf16),
            pltpu.VMEM((2 * cols, nodes), bf16),
            pltpu.VMEM((nodes, cols), bf16),
            pltpu.VMEM((nodes, cols), f32),
            pltpu.VMEM((chips, ys, zs, tall, wide), bf16),
            pltpu.VMEM((chips, ys, zs, tall, wide), bf16),
            pltpu.VMEM((chips, zs, tall, wide), bf16),
            pltpu.VMEM((chips, zs, tall, wide), bf16),
            pltpu.VMEM((chips, zs, tall, wide), bf16),
            pltpu.VMEM((chips, ys, zs, tall, wide), bf16),
            dma((parts,)), dma((parts,)), dma((parts,)), dma((parts,)), dma((parts,)), dma((parts,)),
            dma((5,)), dma((CHUNKS,)), dma((2,)), dma((parts,)),
            dma((3, hops, CHUNKS)), dma((3, CHUNKS)), dma((3, hops, CHUNKS)), dma((3, feats, CHUNKS)),
            dma((chips, ys)), dma((chips, ys)), dma((chips, zs)), dma((chips, zs)),
            dma((chips, zs)), dma((chips, zs)), dma((chips, ys)), dma((chips, ys)),
        ],
        compiler_params=pltpu.CompilerParams(
            collective_id=0, has_side_effects=True, vmem_limit_bytes=VMEM_BYTES
        ),
        name="layer",
    )(send_counts, outgoing, send_rows, degrees, features, cotangent, w_self, w_neigh)


def on_device(
    features,
    w_self,
    w_neigh,
    adjacency,
    block_source,
    block_to_slot,
    send_rows,
    send_counts,
    degree,
    cotangent,
):
    part_count = lax.axis_size("graph")
    feat_cols = features.shape[1]
    block_size = adjacency.shape[1]
    slot_cap = send_rows.shape[2]
    slot_total = part_count * slot_cap // block_size
    outgoing = collect(block_source, block_to_slot, send_counts, adjacency, features, slot_total)
    hidden, returned, self_grad, grad_self, grad_neigh = layer(
        send_counts, outgoing.reshape(part_count, slot_cap, feat_cols), send_rows,
        degree.reshape(-1, block_size), features, cotangent, w_self, w_neigh,
    )
    grad_features, hidden_out, grad_self, grad_neigh = spread(
        block_source, block_to_slot, adjacency,
        returned.reshape(slot_total, block_size, feat_cols), self_grad, hidden, grad_self, grad_neigh,
    )
    return (hidden_out, grad_features, grad_self, grad_neigh)


def solution(mesh):
    placed = (
        P("graph", "feat"),
        P(),
        P(),
        P("graph", None, None),
        P("graph"),
        P("graph"),
        P("graph", None, None),
        P("graph", None),
        P("graph"),
        P("graph", "feat"),
    )
    return jax.shard_map(
        on_device,
        mesh=mesh,
        in_specs=placed,
        out_specs=(P("graph", "feat"), P("graph", "feat"), P("feat", None), P("feat", None)),
        check_vma=False,
    )
```
